32 devices in a mesh: scen: 4 (over z), line: 8 (over y, x, core).
Axes of the slice: x: 2, y: 2, z: 4, core: 2. Of those that a mesh axis runs over, the one named last changes fastest.
Arguments:
- shift_factors: bfloat16 [32768, 20480], P('line', 'scen'), may hold values from -0.0390625 to 0.0390625
- gen_bus: int32 [4096], P('scen'), may hold values from 0 to 20479, as said below
- commit: int32 [4096], P('scen'), may hold values 0 or 1
- cost_coef: float32 [2, 4096], P(None, 'scen'), may hold values from 0.2 to 2
- gen_cap: float32 [4096], P('scen'), may hold values from 0.5 to 4
- bus_loads: float32 [48, 20480], P('line', 'scen'), may hold values from 0.04 to 6
- load_shed: float32 [48, 20480], P('line', 'scen'), may hold values from 0 to 0.3
- dispatch: float32 [48, 4096], P('line', 'scen'), may hold values from 0 to 2
- ph_dual: float32 [48, 4096], P('line', 'scen'), may hold values from -3 to 3
- consensus_prev: float32 [4096], P('scen'), may hold values from 0 to 2
- scen_weight: float32 [48], P('line'), may hold values from 1 to 150000
- flow_copy: float32 [48, 32768], P('scen', 'line'), may hold values from -5 to 5
- flow_dual: float32 [48, 32768], P('scen', 'line'), may hold values from -1.75 to 1.75
- balance_dual: float32 [48], P('line'), may hold values from -3 to 3
- flow_limit: float32 [32768], P('line'), may hold values from 0.4 to 2
Outputs:
- dispatch_out: float32 [48, 4096], P('line', 'scen')
- shed_out: float32 [48, 20480], P('line', 'scen')
- flow_copy_out: float32 [48, 32768], P('scen', 'line')
- flow_dual_out: float32 [48, 32768], P('scen', 'line')
- balance_dual_out: float32 [48], P('line')
- consensus: float32 [4096], P('scen')
- ph_dual_out: float32 [48, 4096], P('line', 'scen')
The draws below stay inside these ranges and needn't reach their ends.
Inputs may be any that keep to these rules, and one draw needn't show every extreme that they name: `gen_bus`: generator j sits at one of the buses j * (5) to (j + 1) * 5 - 1, so no two generators share a bus.
All inputs are finite; a program needn't handle non-finite values. No bound on the sum of `commit` on one device may be relied on, other than what follows from the above.
Results may differ from the reference program's by a relative error of at most 0.0056.
Values may be sent and summed in bfloat16 or wider, within the bound.
No kernel may reach another device: no remote copies, remote signals or barrier semaphores. Data moves between devices by JAX's collectives and lax.ppermute only.
A program may use at most 128 MiB of HBM per device.

```python
import math
import jax
import jax.numpy as jnp
from jax import lax

BUSES = 20480
LINES = 32768
GENS = 4096
ITERS = 2
SCENARIOS = 48
N_LINE = 8


def draw_gen_bus(key, part):
    stretch = BUSES // GENS
    offsets = jax.random.randint(key, (GENS,), 0, stretch)
    offsets = offsets.at[0].set(0).at[GENS - 1].set(stretch - 1)
    return (jnp.arange(GENS, dtype=jnp.int32) * stretch + offsets).astype(jnp.int32)


def draw_bus_loads(key, part):
    first_key = jax.random.fold_in(key, 11)
    second_key = jax.random.fold_in(key, 12)
    region = 1.0 + 2.0 * jnp.arange(BUSES, dtype=jnp.float32) / BUSES
    baseline = jax.random.uniform(first_key, (SCENARIOS, BUSES), jnp.float32, 0.3, 1.0)
    scenario_level = jnp.exp(jax.random.uniform(second_key, (SCENARIOS, 1), jnp.float32, math.log(0.7), math.log(1.4)))
    return (baseline * region[None, :] * scenario_level).astype(jnp.float32)


def draw_scen_weight(key, part):
    rising = 1.0 + 4.0 * jnp.arange(SCENARIOS, dtype=jnp.float32) / SCENARIOS
    baseline = jnp.exp(jax.random.uniform(key, (SCENARIOS,), jnp.float32, 0.0, math.log(10000.0)))
    return (baseline * rising).astype(jnp.float32)


def with_ends(drawn, own_key, least, high):
    longest = drawn.shape.index(max(drawn.shape))
    spots = []
    for shift in (0, 1):
        where = [jax.random.randint(jax.random.fold_in(own_key, axis), (), 0, length) for axis, length in enumerate(drawn.shape)]
        where[longest] = (where[longest] + shift) % drawn.shape[longest]
        spots.append(tuple(where))
    return drawn.at[spots[0]].set(least).at[spots[1]].set(high)


def block_levels(own_key, shape, split, smallest, top_value):
    level = 1.0
    for dim, blocks in split:
        steps = jax.random.uniform(jax.random.fold_in(jax.random.fold_in(own_key, 6), dim), (blocks,), jnp.float32, smallest / len(split), top_value / len(split))
        level = level * jnp.repeat(jnp.exp(steps), shape[dim] // blocks).reshape((-1,) + (1,) * (len(shape) - 1 - dim))
    return level


def normal_values(rng, extent, scale, limit, split=(), kind=jnp.bfloat16):
    result = jax.random.normal(rng, extent, jnp.float32) * scale
    if len(split) > 0:
        result = block_levels(rng, extent, split, -0.22, 0.18) * result
    return jnp.clip(result, min=-limit, max=limit).astype(kind)


def setup_inputs(seed: int = 0) -> dict:
    arg_keys = jax.random.split(jax.random.key(seed), 16)
    return {
        "shift_factors": normal_values(arg_keys[0], (LINES, BUSES), BUSES ** -0.5, 0.0390625, ((0, 8), (1, 4))),
        "gen_bus": draw_gen_bus(jax.random.fold_in(arg_keys[15], 71), 0),
        "commit": with_ends((jax.random.randint(arg_keys[2], (GENS,), 0, 4) < 3).astype(jnp.int32), jax.random.fold_in(arg_keys[2], 1), 0, 1),
        "cost_coef": jnp.clip(jnp.exp(math.log(2.0) - 2.3025851 * jax.random.uniform(arg_keys[3], (2, GENS), jnp.float32) ** block_levels(arg_keys[3], (2, GENS), ((1, 4),), -0.2, 0.2)), 0.2, 2.0),
        "gen_cap": jnp.clip(jnp.exp(math.log(4.0) - 2.0794415 * jax.random.uniform(arg_keys[4], (GENS,), jnp.float32) ** block_levels(arg_keys[4], (GENS,), ((0, 4),), -0.2, 0.2)), 0.5, 4.0),
        "bus_loads": draw_bus_loads(jax.random.fold_in(arg_keys[15], 71), 0),
        "load_shed": jnp.clip(0.3 * jax.random.uniform(arg_keys[6], (SCENARIOS, BUSES), jnp.float32) ** block_levels(arg_keys[6], (SCENARIOS, BUSES), ((0, 8), (1, 4)), -0.2, 0.2), 0.0, 0.3),
        "dispatch": jnp.clip(2.0 * jax.random.uniform(arg_keys[7], (SCENARIOS, GENS), jnp.float32) ** block_levels(arg_keys[7], (SCENARIOS, GENS), ((0, 8), (1, 4)), -0.2, 0.2), 0.0, 2.0),
        "ph_dual": normal_values(arg_keys[8], (SCENARIOS, GENS), 0.5, 3.0, ((0, 8), (1, 4)), jnp.float32),
        "consensus_prev": jnp.clip(2.0 * jax.random.uniform(arg_keys[9], (GENS,), jnp.float32) ** block_levels(arg_keys[9], (GENS,), ((0, 4),), -0.2, 0.2), 0.0, 2.0),
        "scen_weight": draw_scen_weight(jax.random.fold_in(arg_keys[15], 71), 0),
        "flow_copy": normal_values(arg_keys[11], (SCENARIOS, LINES), 0.8, 5.0, ((0, 4), (1, 8)), jnp.float32),
        "flow_dual": normal_values(arg_keys[12], (SCENARIOS, LINES), 0.3, 1.75, ((0, 4), (1, 8)), jnp.float32),
        "balance_dual": normal_values(arg_keys[13], (SCENARIOS,), 0.5, 3.0, ((0, 8),), jnp.float32),
        "flow_limit": jnp.clip(jnp.exp(math.log(2.0) - 1.609438 * jax.random.uniform(arg_keys[14], (LINES,), jnp.float32) ** block_levels(arg_keys[14], (LINES,), ((0, 8),), -0.2, 0.2)), 0.4, 2.0),
    }


def reference(shift_factors, gen_bus, commit, cost_coef, gen_cap, bus_loads, load_shed, dispatch, ph_dual, consensus_prev, scen_weight, flow_copy, flow_dual, balance_dual, flow_limit):
    line_blocks = shift_factors.reshape(N_LINE, LINES // N_LINE, BUSES)
    capacity = gen_cap * commit.astype(jnp.float32)
    generation = dispatch
    served = load_shed
    copy_now = flow_copy
    dual_now = flow_dual
    bal_dual = balance_dual
    for iteration in range(ITERS):
        placed = jnp.zeros((SCENARIOS, BUSES), jnp.float32).at[:, gen_bus].add(generation)
        inject = (placed + served - bus_loads).astype(jnp.bfloat16)
        inject_wide = inject.astype(jnp.float32)

        def forward(line_block):
            return lax.dot_general(inject_wide, line_block.astype(jnp.float32), (((1,), (1,)), ((), ())), precision=lax.Precision.HIGHEST, preferred_element_type=jnp.float32)

        flows_now = jnp.transpose(lax.map(forward, line_blocks), (1, 0, 2)).reshape(SCENARIOS, LINES)
        balance = jnp.sum(inject_wide, axis=1) / BUSES
        residual = (flows_now - copy_now + dual_now).astype(jnp.bfloat16)
        residual_blocks = jnp.transpose(residual.reshape(SCENARIOS, N_LINE, LINES // N_LINE), (1, 0, 2))

        def backward(running_sum, operands):
            partial_term = jnp.dot(operands[0].astype(jnp.float32), operands[1].astype(jnp.float32), precision=lax.Precision.HIGHEST, preferred_element_type=jnp.float32)
            return running_sum + partial_term, None

        bus_sum, unused = lax.scan(backward, jnp.zeros((SCENARIOS, BUSES), jnp.float32), (residual_blocks, line_blocks))
        bus_grad = bus_sum + (balance + bal_dual)[:, None]
        gen_grad = cost_coef[0] + cost_coef[1] * generation + ph_dual + (generation - consensus_prev) + bus_grad[:, gen_bus]
        generation = jnp.minimum(jnp.maximum(generation - 0.4 * gen_grad, 0.0), capacity[None, :])
        served = jnp.minimum(jnp.maximum(served - 0.4 * (1.5 + bus_grad), 0.0), bus_loads)
        copy_next = jnp.minimum(jnp.maximum(flows_now + dual_now, -flow_limit[None, :]), flow_limit[None, :])
        dual_now = dual_now + flows_now - copy_next
        copy_now = copy_next
        bal_dual = bal_dual + balance
    weight_total = jnp.sum(scen_weight)
    consensus = jnp.sum(scen_weight[:, None] * generation, axis=0) / weight_total
    return (generation, served, copy_now, dual_now, bal_dual, consensus, ph_dual + (generation - consensus))
```

```python
import functools

import jax
import jax.numpy as jnp
from jax import lax
from jax.experimental import pallas as pl
from jax.experimental.pallas import tpu as pltpu
from jax.sharding import PartitionSpec as P

BUSES = 20480
ITERS = 2
CHUNKS = 1
LANES = 128
BF = jnp.bfloat16
F32 = jnp.float32
WHOLE = pl.BlockSpec(memory_space=pltpu.VMEM)


def call(kernel, args, outs, scratch=(), flops=0):
    size = sum(a.size * a.dtype.itemsize for a in args)
    return pl.pallas_call(
        kernel,
        in_specs=[WHOLE] * len(args),
        out_specs=[WHOLE] * len(outs),
        out_shape=[jax.ShapeDtypeStruct(shape, kind) for shape, kind in outs],
        scratch_shapes=[pltpu.VMEM(shape, kind) for shape, kind in scratch],
        compiler_params=pltpu.CompilerParams(vmem_limit_bytes=10 << 20),
        cost_estimate=pl.CostEstimate(flops=flops, bytes_accessed=size, transcendentals=0),
    )(*args)


def pieces(value):
    high = value.astype(BF)
    rest = value - high.astype(F32)
    middle = rest.astype(BF)
    low = (rest - middle.astype(F32)).astype(BF)
    return high, middle, low


def dot_t(a, b):
    return lax.dot_general(a, b, (((1,), (1,)), ((), ())), preferred_element_type=F32)


class Sizes:
    def __init__(self, mesh, lines, buses, gens, rows):
        self.scen = mesh.shape["scen"]
        self.line = mesh.shape["line"]
        self.chips = self.line // 2
        assert self.chips == self.scen
        self.lines, self.buses, self.gens, self.rows = lines, buses, gens, rows
        self.pair = 2 * rows
        self.total = rows * self.line
        self.stretch = buses // gens
        self.width = self.stretch * LANES
        self.fold = next(f for f in (4, 2, 1) if buses % (f * self.width) == 0)
        self.part = buses // self.fold
        self.chunk = lines // CHUNKS
        self.half = self.chunk // 2


def where_am_i():
    line = lax.axis_index("line")
    return lax.axis_index("scen"), lax.div(line, 2), lax.rem(line, 2)


def place(sz, gens, select, block):
    spread = select[block]
    high, middle, low = pieces(gens)
    return (dot_t(low, spread) + dot_t(middle, spread)) + dot_t(high, spread)


def blocks_of(sz):
    per = sz.part // sz.width
    for block in range(sz.gens // LANES):
        fold, inner = divmod(block, per)
        yield block, slice(fold * sz.rows, (fold + 1) * sz.rows), slice(inner * sz.width, (inner + 1) * sz.width)


def start_kernel(sz, dispatch, shed, loads, gen_bus, inject, shed_p, loads_p, select):
    first = lax.axis_index("scen") * sz.buses
    bus = lax.broadcasted_iota(jnp.int32, (sz.width, LANES), 0)
    for block, rows, cols in blocks_of(sz):
        lanes = slice(block * LANES, (block + 1) * LANES)
        buses = slice(block * sz.width, (block + 1) * sz.width)
        local = gen_bus[:, lanes] - (first + block * sz.width)
        select[block] = (bus == local).astype(F32).astype(BF)
        here, load = shed[:, buses], loads[:, buses]
        inject[rows, cols] = (place(sz, dispatch[:, lanes], select, block) + here - load).astype(BF)
        shed_p[rows, cols] = here
        loads_p[rows, cols] = load


def forward_kernel(sz, chunk, step, *refs):
    chips = sz.chips
    own, other = refs[:chips], refs[chips : 2 * chips]
    factors = refs[2 * chips]
    outs = refs[2 * chips + 1 : 3 * chips + 1]
    inject, flows = refs[3 * chips + 1 :]
    scen, chip, core = where_am_i()
    extra = LANES if chunk == 0 else 0

    def gather(first, second):
        for slot in range(chips):
            for fold in range(sz.fold):
                rows = slice(fold * sz.rows, (fold + 1) * sz.rows)
                cols = slice(fold * sz.part, (fold + 1) * sz.part)
                base = slot * sz.pair
                inject[base : base + sz.rows, cols] = first[slot][rows, :]
                inject[base + sz.rows : base + sz.pair, cols] = second[slot][rows, :]

    @pl.when(core == 0)
    def _():
        gather(own, other)

    @pl.when(core == 1)
    def _():
        gather(other, own)

    if extra:
        total = jnp.sum(inject[...].astype(F32), axis=1, keepdims=True)
        high, middle, low = (piece.astype(F32) for piece in pieces(total))
        lane = lax.broadcasted_iota(jnp.int32, (sz.total, LANES), 1)
        tile = jnp.where(lane == 0, high, jnp.where(lane == 1, middle, jnp.where(lane == 2, low, 0.0)))
        for slot in range(chips):
            flows[slot, :, sz.half :] = jnp.zeros((2 * sz.pair, LANES), F32)
            flows[slot, : sz.pair, sz.half :] = tile[slot * sz.pair : (slot + 1) * sz.pair]
    for side in range(2):

        def body(i, _, side=side):
            source = pl.ds(pl.multiple_of(chunk * sz.chunk + side * sz.half + i * step, step), step)
            target = pl.ds(pl.multiple_of(i * step, step), step)
            product = dot_t(inject[...], factors[source, :])
            for slot in range(chips):
                flows[slot, side * sz.pair : (side + 1) * sz.pair, target] = product[
                    slot * sz.pair : (slot + 1) * sz.pair
                ]
            return 0

        lax.fori_loop(0, sz.half // step, body, 0)
    for away in range(chips):
        found = flows[chip ^ scen ^ away]
        outs[away][...] = found.astype(outs[away].dtype)


def residual_kernel(sz, chunk, join, *refs):
    scen = sz.scen
    parts = refs[:scen]
    copies, duals, limits = refs[scen : scen + 3]
    old = refs[scen + 3 : scen + 5] if join else None
    residual, copy_out, dual_out = refs[-3:]
    total = parts[0][...]
    for part in parts[1:]:
        total = total + part[...].astype(F32)
    for side in range(2):
        rows = slice(side * sz.pair, (side + 1) * sz.pair)
        start = chunk * sz.chunk + side * sz.half
        base = chunk * sz.chunk if copies.shape[1] == sz.lines else 0
        cols = slice(base + side * sz.half, base + (side + 1) * sz.half)
        to = slice(start, start + sz.half) if join else slice(side * sz.half, (side + 1) * sz.half)
        now, copy, dual = total[rows, : sz.half], copies[:, cols], duals[:, cols]
        limit = limits[:, start : start + sz.half]
        residual[rows, : sz.half] = (now - copy + dual).astype(BF)
        copy_next = jnp.minimum(jnp.maximum(now + dual, -limit), limit)
        copy_out[:, to] = copy_next
        dual_out[:, to] = dual + now - copy_next
    if join:
        copy_out[:, : chunk * sz.chunk] = old[0][...]
        dual_out[:, : chunk * sz.chunk] = old[1][...]
    if chunk == 0:
        balance = jnp.sum(total[:, sz.half :], axis=1, keepdims=True) / BUSES
        high, middle, low = (piece.astype(F32) for piece in pieces(balance))
        lane = lax.broadcasted_iota(jnp.int32, (2 * sz.pair, LANES), 1)
        tile = jnp.where(lane == 0, high, jnp.where(lane == 1, middle, jnp.where(lane == 2, low, 0.0)))
        residual[:, sz.half :] = tile.astype(BF)


def backward_kernel(sz, chunk, step, *refs):
    scen = sz.scen
    parts, factors = refs[:scen], refs[scen]
    before = refs[scen + 1] if chunk else None
    last = chunk == CHUNKS - 1
    residual = refs[-1]
    outs = refs[scen + 1 + (chunk > 0) : -1]
    me, chip, core = where_am_i()
    if chunk == 0:
        balances = outs[-1]
        for slot in range(scen):

            @pl.when(chip == (me ^ slot))
            def _(slot=slot):
                tile = parts[slot][: sz.pair, sz.half :].astype(F32)
                found = jnp.sum(tile, axis=1, keepdims=True)
                balances[...] = jnp.broadcast_to(found, (sz.pair, LANES))

    for slot in range(scen):
        for side in range(2):
            residual[slot * sz.pair : (slot + 1) * sz.pair, side * sz.half : (side + 1) * sz.half] = parts[slot][
                side * sz.pair : (side + 1) * sz.pair, : sz.half
            ]

    def body(i, _):
        cols = pl.ds(pl.multiple_of(i * step, step), step)
        product = jnp.dot(
            residual[...],
            factors[chunk * sz.chunk : (chunk + 1) * sz.chunk, cols],
            preferred_element_type=F32,
        )
        if chunk:
            product = before[:, cols] + product
        if not last:
            outs[0][:, cols] = product
            return 0
        kept, sent = outs[:2]
        even = [product[slot * sz.pair : slot * sz.pair + sz.rows] for slot in range(scen)]
        odd = [product[slot * sz.pair + sz.rows : (slot + 1) * sz.pair] for slot in range(scen)]
        even, odd = jnp.concatenate(even, 0), jnp.concatenate(odd, 0)
        kept[:, cols] = jnp.where(core == 0, even, odd)
        sent[:, cols] = jnp.where(core == 0, odd, even).astype(BF)
        return 0

    lax.fori_loop(0, sz.buses // step, body, 0)


def chip_kernel(sz, *refs):
    kept, received = refs[:2]
    outs, packed = refs[2:-1], refs[-1]
    scen, chip, core = where_am_i()
    total = kept[...] + received[...].astype(F32)
    for slot in range(sz.scen):
        for fold in range(sz.fold):
            packed[slot, fold * sz.rows : (fold + 1) * sz.rows, :] = total[
                slot * sz.rows : (slot + 1) * sz.rows, fold * sz.part : (fold + 1) * sz.part
            ]
    for away in range(sz.chips):
        found = packed[scen ^ chip ^ away]
        outs[away][...] = found.astype(outs[away].dtype)


def update_kernel(sz, last, *refs):
    parts = refs[: sz.chips]
    balances, lam, shed, loads, gens, select, costs, dual, previous, cap, commit = refs[sz.chips : sz.chips + 11]
    rest = refs[sz.chips + 11 :]
    core = where_am_i()[2]
    balance = jnp.where(core == 0, balances[: sz.rows, :1], balances[sz.rows :, :1])
    lam_now = lam[:, :1]
    shift = balance + lam_now
    shift = jnp.concatenate([shift] * sz.fold, 0)
    total = parts[0][...]
    for part in parts[1:]:
        total = total + part[...].astype(F32)
    grad = total + shift
    shed_next = jnp.minimum(jnp.maximum(shed[...] - 0.4 * (1.5 + grad), 0.0), loads[...])
    capacity = cap[...] * commit[...].astype(F32)
    if last:
        weights, gens_out, shed_out, lam_out, weighted_out = rest
    else:
        gens_out, shed_out, lam_out, inject = rest
        shed_out[...] = shed_next
    lam_out[...] = jnp.broadcast_to(lam_now + balance, lam_out.shape)
    for block, rows, cols in blocks_of(sz):
        lanes = slice(block * LANES, (block + 1) * LANES)
        spread = select[block]
        high, middle, low = (
            jnp.dot(piece, spread, preferred_element_type=F32) for piece in pieces(grad[rows, cols])
        )
        picked = (low + middle) + high
        now = gens[:, lanes]
        gen_grad = costs[:1, lanes] + costs[1:, lanes] * now + dual[:, lanes] + (now - previous[:, lanes]) + picked
        now = jnp.minimum(jnp.maximum(now - 0.4 * gen_grad, 0.0), capacity[:, lanes])
        gens_out[:, lanes] = now
        if last:
            shed_out[:, block * sz.width : (block + 1) * sz.width] = shed_next[rows, cols]
            weighted_out[:1, lanes] = jnp.sum(weights[:, :1] * now, axis=0, keepdims=True)
            all_weights = jnp.sum(weights[:, :1], axis=0, keepdims=True)
            weighted_out[1:, lanes] = jnp.broadcast_to(all_weights, (7, LANES))
        else:
            inject[rows, cols] = (
                place(sz, now, select, block) + shed_next[rows, cols] - loads[rows, cols]
            ).astype(BF)


def add_kernel(first, second, out):
    out[...] = first[...] + second[...]


def finish_kernel(sz, *refs):
    parts = refs[: sz.chips]
    dual, gens, consensus, dual_out = refs[sz.chips :]
    total = parts[0][...]
    for part in parts[1:]:
        total = total + part[...]
    mean = total[:1] / total[1:2]
    consensus[...] = mean
    dual_out[...] = dual[...] + (gens[...] - mean)


def to_scen(n, away, value):
    return lax.ppermute(value, "scen", [(i, i ^ away) for i in range(n)])


def to_chip(n, away, value):
    return lax.ppermute(value, "line", [(i, i ^ (2 * away)) for i in range(n)])


def to_core(n, value):
    return lax.ppermute(value, "line", [(i, i ^ 1) for i in range(n)])


def local(
    mesh,
    shift_factors,
    gen_bus,
    commit,
    cost_coef,
    gen_cap,
    bus_loads,
    load_shed,
    dispatch,
    ph_dual,
    consensus_prev,
    scen_weight,
    flow_copy,
    flow_dual,
    balance_dual,
    flow_limit,
):
    lines, buses = shift_factors.shape
    rows, gens = dispatch.shape
    sz = Sizes(mesh, lines, buses, gens, rows)
    n_scen, n_line, chips = sz.scen, sz.line, sz.chips
    row = lambda v: v.reshape(1, -1)
    column = lambda v: jnp.broadcast_to(v[:, None], (rows, LANES))
    capacity, on, previous, limits = row(gen_cap), row(commit), row(consensus_prev), row(flow_limit)
    lam, weights = column(balance_dual), column(scen_weight)
    packed = (sz.fold * rows, sz.part)
    step_f = min(512, sz.half)
    step_b = next(s for s in (1024, 640, 512, 256, 128) if buses % s == 0)
    macs = sz.total * sz.chunk * buses

    generation, copies, duals = dispatch, flow_copy, flow_dual
    inject, shed, loads, select = call(
        functools.partial(start_kernel, sz),
        (dispatch, load_shed, bus_loads, row(gen_bus)),
        (
            (packed, BF),
            (packed, F32),
            (packed, F32),
            ((gens // LANES, sz.width, LANES), BF),
        ),
    )
    for iteration in range(ITERS):
        own = [inject] + [to_chip(n_line, away, inject) for away in range(1, chips)]
        other = [to_core(n_line, value) for value in own]
        residuals, new_copies, new_duals = [], [], []
        final = iteration == ITERS - 1
        for chunk in range(CHUNKS):
            block = (2 * sz.pair, sz.half + (LANES if chunk == 0 else 0))
            flows = call(
                functools.partial(forward_kernel, sz, chunk, step_f),
                (*own, *other, shift_factors),
                [(block, F32)] + [(block, BF)] * (chips - 1),
                [((sz.total, buses), BF), ((chips, *block), F32)],
                flops=2 * macs,
            )
            parts = [flows[0]] + [to_scen(n_scen, away, flows[away]) for away in range(1, n_scen)]
            join = final and chunk == CHUNKS - 1 and CHUNKS > 1
            width = lines if join else sz.chunk
            whole = iteration == 0
            residual, copy_next, dual_next = call(
                functools.partial(residual_kernel, sz, chunk, join),
                (
                    *parts,
                    flow_copy if whole else copies[chunk],
                    flow_dual if whole else duals[chunk],
                    limits,
                    *((new_copies[0], new_duals[0]) if join else ()),
                ),
                [(block, BF), ((sz.pair, width), F32), ((sz.pair, width), F32)],
            )
            new_copies.append(copy_next)
            new_duals.append(dual_next)
            residuals.append([residual] + [to_scen(n_scen, away, residual) for away in range(1, n_scen)])
        copies, duals = new_copies, new_duals
        before, balances = (), None
        for chunk in range(CHUNKS):
            last = chunk == CHUNKS - 1
            half = (sz.total // 2, buses)
            outs = [(half, F32), (half, BF)] if last else [((sz.total, buses), F32)]
            if chunk == 0:
                outs.append(((sz.pair, LANES), F32))
            found = call(
                functools.partial(backward_kernel, sz, chunk, step_b),
                (*residuals[chunk], shift_factors, *before),
                outs,
                [((sz.total, sz.chunk), BF)],
                flops=2 * macs,
            )
            if chunk == 0:
                balances = found[-1]
            before = found[:1]
        kept, sent = found[:2]
        sums = call(
            functools.partial(chip_kernel, sz),
            (kept, to_core(n_line, sent)),
            [(packed, F32)] + [(packed, BF)] * (chips - 1),
            [((chips, *packed), F32)],
        )
        parts = [sums[0]] + [to_chip(n_line, away, sums[away]) for away in range(1, chips)]
        args = (*parts, balances, lam, shed, loads, generation, select, cost_coef, ph_dual, previous, capacity, on)
        if not final:
            generation, shed, lam, inject = call(
                functools.partial(update_kernel, sz, False),
                args,
                [((rows, gens), F32), (packed, F32), ((rows, LANES), F32), (packed, BF)],
            )
        else:
            generation, shed, lam, weighted = call(
                functools.partial(update_kernel, sz, True),
                (*args, weights),
                [((rows, gens), F32), ((rows, buses), F32), ((rows, LANES), F32), ((8, gens), F32)],
            )
    (weighted,) = call(add_kernel, (weighted, to_core(n_line, weighted)), [((8, gens), F32)])
    parts = [weighted] + [to_chip(n_line, away, weighted) for away in range(1, chips)]
    consensus, dual_out = call(
        functools.partial(finish_kernel, sz),
        (*parts, ph_dual, generation),
        [((1, gens), F32), ((rows, gens), F32)],
    )
    return generation, shed, copies[-1], duals[-1], lam[:, 0], consensus.reshape(-1), dual_out


def solution(mesh):
    return jax.shard_map(
        functools.partial(local, mesh),
        mesh=mesh,
        in_specs=(
            P("line", "scen"),
            P("scen"),
            P("scen"),
            P(None, "scen"),
            P("scen"),
            P("line", "scen"),
            P("line", "scen"),
            P("line", "scen"),
            P("line", "scen"),
            P("scen"),
            P("line"),
            P("scen", "line"),
            P("scen", "line"),
            P("line"),
            P("line"),
        ),
        out_specs=(
            P("line", "scen"),
            P("line", "scen"),
            P("scen", "line"),
            P("scen", "line"),
            P("line"),
            P("scen"),
            P("line", "scen"),
        ),
        check_vma=False,
    )
```

```python
import functools
import math

import jax
import jax.numpy as jnp
from jax import lax
from jax.experimental import pallas as pl
from jax.experimental.pallas import tpu as pltpu
from jax.sharding import PartitionSpec as P

BUSES = 20480
ITERS = 2
CHUNKS = 1
LANES = 128
GRANT = 11 << 20
BF = jnp.bfloat16
F32 = jnp.float32
WHOLE = pl.BlockSpec(memory_space=pltpu.VMEM)


def call(kernel, args, outs, scratch=(), flops=0, keep=None, limit=GRANT):
    size = sum(a.size * a.dtype.itemsize for a in args)
    if keep is not None:
        inner, args = kernel, (keep, *args)
        kernel = lambda kept, *refs: inner(*refs)
    return pl.pallas_call(
        kernel,
        in_specs=[WHOLE] * len(args),
        out_specs=[WHOLE] * len(outs),
        out_shape=[jax.ShapeDtypeStruct(shape, kind) for shape, kind in outs],
        scratch_shapes=[pltpu.VMEM(shape, kind) for shape, kind in scratch],
        compiler_params=pltpu.CompilerParams(vmem_limit_bytes=limit),
        cost_estimate=pl.CostEstimate(flops=flops, bytes_accessed=size, transcendentals=0),
    )(*args)


def nbytes(arrays):
    size = lambda a: math.prod(a.shape[:-2]) * -(-a.shape[-2] // 8) * 8 * a.shape[-1] * a.dtype.itemsize
    return sum(size(a) for a in arrays)


def pieces(value):
    high = value.astype(BF)
    rest = value - high.astype(F32)
    middle = rest.astype(BF)
    low = (rest - middle.astype(F32)).astype(BF)
    return high, middle, low


def dot_t(a, b):
    return lax.dot_general(a, b, (((1,), (1,)), ((), ())), preferred_element_type=F32)


class Sizes:
    def __init__(self, mesh, lines, buses, gens, rows):
        self.scen = mesh.shape["scen"]
        self.line = mesh.shape["line"]
        self.chips = self.line // 2
        assert self.chips == self.scen
        self.lines, self.buses, self.gens, self.rows = lines, buses, gens, rows
        self.pair = 2 * rows
        self.total = rows * self.line
        self.stretch = buses // gens
        self.width = self.stretch * LANES
        self.fold = next(f for f in (4, 2, 1) if buses % (f * self.width) == 0)
        self.part = buses // self.fold
        self.chunk = lines // CHUNKS
        self.half = self.chunk // 2


def where_am_i():
    line = lax.axis_index("line")
    return lax.axis_index("scen"), lax.div(line, 2), lax.rem(line, 2)


def place(sz, gens, select, block):
    spread = select[block]
    high, middle, low = pieces(gens)
    return (dot_t(low, spread) + dot_t(middle, spread)) + dot_t(high, spread)


def blocks_of(sz):
    per = sz.part // sz.width
    for block in range(sz.gens // LANES):
        fold, inner = divmod(block, per)
        yield block, slice(fold * sz.rows, (fold + 1) * sz.rows), slice(inner * sz.width, (inner + 1) * sz.width)


def start_kernel(sz, dispatch, shed, loads, gen_bus, inject, shed_p, loads_p, select):
    first = lax.axis_index("scen") * sz.buses
    bus = lax.broadcasted_iota(jnp.int32, (sz.width, LANES), 0)
    for block, rows, cols in blocks_of(sz):
        lanes = slice(block * LANES, (block + 1) * LANES)
        buses = slice(block * sz.width, (block + 1) * sz.width)
        local = gen_bus[:, lanes] - (first + block * sz.width)
        select[block] = (bus == local).astype(F32).astype(BF)
        here, load = shed[:, buses], loads[:, buses]
        inject[rows, cols] = (place(sz, dispatch[:, lanes], select, block) + here - load).astype(BF)
        shed_p[rows, cols] = here
        loads_p[rows, cols] = load


def forward_kernel(sz, chunk, step, *refs):
    chips = sz.chips
    own, other = refs[:chips], refs[chips : 2 * chips]
    factors = refs[2 * chips]
    outs = refs[2 * chips + 1 : 3 * chips + 1]
    inject, flows = refs[3 * chips + 1 :]
    scen, chip, core = where_am_i()
    extra = LANES if chunk == 0 else 0

    def gather(first, second):
        for slot in range(chips):
            for fold in range(sz.fold):
                rows = slice(fold * sz.rows, (fold + 1) * sz.rows)
                cols = slice(fold * sz.part, (fold + 1) * sz.part)
                base = slot * sz.pair
                inject[base : base + sz.rows, cols] = first[slot][rows, :]
                inject[base + sz.rows : base + sz.pair, cols] = second[slot][rows, :]

    @pl.when(core == 0)
    def _():
        gather(own, other)

    @pl.when(core == 1)
    def _():
        gather(other, own)

    if extra:
        total = jnp.sum(inject[...].astype(F32), axis=1, keepdims=True)
        high, middle, low = (piece.astype(F32) for piece in pieces(total))
        lane = lax.broadcasted_iota(jnp.int32, (sz.total, LANES), 1)
        tile = jnp.where(lane == 0, high, jnp.where(lane == 1, middle, jnp.where(lane == 2, low, 0.0)))
        for slot in range(chips):
            flows[slot, :, sz.half :] = jnp.zeros((2 * sz.pair, LANES), F32)
            flows[slot, : sz.pair, sz.half :] = tile[slot * sz.pair : (slot + 1) * sz.pair]
    for side in range(2):

        def body(i, _, side=side):
            source = pl.ds(pl.multiple_of(chunk * sz.chunk + side * sz.half + i * step, step), step)
            target = pl.ds(pl.multiple_of(i * step, step), step)
            product = dot_t(inject[...], factors[source, :])
            for slot in range(chips):
                flows[slot, side * sz.pair : (side + 1) * sz.pair, target] = product[
                    slot * sz.pair : (slot + 1) * sz.pair
                ]
            return 0

        lax.fori_loop(0, sz.half // step, body, 0)
    for away in range(chips):
        found = flows[chip ^ scen ^ away]
        outs[away][...] = found.astype(outs[away].dtype)


def residual_kernel(sz, chunk, join, *refs):
    scen = sz.scen
    parts = refs[:scen]
    copies, duals, limits = refs[scen : scen + 3]
    old = refs[scen + 3 : scen + 5] if join else None
    residual, copy_out, dual_out = refs[-3:]
    total = parts[0][...]
    for part in parts[1:]:
        total = total + part[...].astype(F32)
    for side in range(2):
        rows = slice(side * sz.pair, (side + 1) * sz.pair)
        start = chunk * sz.chunk + side * sz.half
        base = chunk * sz.chunk if copies.shape[1] == sz.lines else 0
        cols = slice(base + side * sz.half, base + (side + 1) * sz.half)
        to = slice(start, start + sz.half) if join else slice(side * sz.half, (side + 1) * sz.half)
        now, copy, dual = total[rows, : sz.half], copies[:, cols], duals[:, cols]
        limit = limits[:, start : start + sz.half]
        residual[rows, : sz.half] = (now - copy + dual).astype(BF)
        copy_next = jnp.minimum(jnp.maximum(now + dual, -limit), limit)
        copy_out[:, to] = copy_next
        dual_out[:, to] = dual + now - copy_next
    if join:
        copy_out[:, : chunk * sz.chunk] = old[0][...]
        dual_out[:, : chunk * sz.chunk] = old[1][...]
    if chunk == 0:
        balance = jnp.sum(total[:, sz.half :], axis=1, keepdims=True) / BUSES
        high, middle, low = (piece.astype(F32) for piece in pieces(balance))
        lane = lax.broadcasted_iota(jnp.int32, (2 * sz.pair, LANES), 1)
        tile = jnp.where(lane == 0, high, jnp.where(lane == 1, middle, jnp.where(lane == 2, low, 0.0)))
        residual[:, sz.half :] = tile.astype(BF)


def backward_kernel(sz, chunk, step, *refs):
    scen = sz.scen
    parts, factors = refs[:scen], refs[scen]
    before = refs[scen + 1] if chunk else None
    last = chunk == CHUNKS - 1
    residual = refs[-1]
    outs = refs[scen + 1 + (chunk > 0) : -1]
    me, chip, core = where_am_i()
    if chunk == 0:
        balances = outs[-1]
        for slot in range(scen):

            @pl.when(chip == (me ^ slot))
            def _(slot=slot):
                tile = parts[slot][: sz.pair, sz.half :].astype(F32)
                found = jnp.sum(tile, axis=1, keepdims=True)
                balances[...] = jnp.broadcast_to(found, (sz.pair, LANES))

    for slot in range(scen):
        for side in range(2):
            residual[slot * sz.pair : (slot + 1) * sz.pair, side * sz.half : (side + 1) * sz.half] = parts[slot][
                side * sz.pair : (side + 1) * sz.pair, : sz.half
            ]

    def body(i, _):
        cols = pl.ds(pl.multiple_of(i * step, step), step)
        product = jnp.dot(
            residual[...],
            factors[chunk * sz.chunk : (chunk + 1) * sz.chunk, cols],
            preferred_element_type=F32,
        )
        if chunk:
            product = before[:, cols] + product
        if not last:
            outs[0][:, cols] = product
            return 0
        kept, sent = outs[:2]
        even = [product[slot * sz.pair : slot * sz.pair + sz.rows] for slot in range(scen)]
        odd = [product[slot * sz.pair + sz.rows : (slot + 1) * sz.pair] for slot in range(scen)]
        even, odd = jnp.concatenate(even, 0), jnp.concatenate(odd, 0)
        kept[:, cols] = jnp.where(core == 0, even, odd)
        sent[:, cols] = jnp.where(core == 0, odd, even).astype(BF)
        return 0

    lax.fori_loop(0, sz.buses // step, body, 0)


def chip_kernel(sz, *refs):
    kept, received = refs[:2]
    outs, packed = refs[2:-1], refs[-1]
    scen, chip, core = where_am_i()
    total = kept[...] + received[...].astype(F32)
    for slot in range(sz.scen):
        for fold in range(sz.fold):
            packed[slot, fold * sz.rows : (fold + 1) * sz.rows, :] = total[
                slot * sz.rows : (slot + 1) * sz.rows, fold * sz.part : (fold + 1) * sz.part
            ]
    for away in range(sz.chips):
        found = packed[scen ^ chip ^ away]
        outs[away][...] = found.astype(outs[away].dtype)


def update_kernel(sz, last, *refs):
    parts = refs[: sz.chips]
    balances, lam, shed, loads, gens, select, costs, dual, previous, cap, commit = refs[sz.chips : sz.chips + 11]
    rest = refs[sz.chips + 11 :]
    core = where_am_i()[2]
    balance = jnp.where(core == 0, balances[: sz.rows, :1], balances[sz.rows :, :1])
    lam_now = lam[:, :1]
    shift = balance + lam_now
    shift = jnp.concatenate([shift] * sz.fold, 0)
    total = parts[0][...]
    for part in parts[1:]:
        total = total + part[...].astype(F32)
    grad = total + shift
    shed_next = jnp.minimum(jnp.maximum(shed[...] - 0.4 * (1.5 + grad), 0.0), loads[...])
    capacity = cap[...] * commit[...].astype(F32)
    if last:
        weights, gens_out, shed_out, lam_out, weighted_out = rest
    else:
        gens_out, shed_out, lam_out, inject = rest
        shed_out[...] = shed_next
    lam_out[...] = jnp.broadcast_to(lam_now + balance, lam_out.shape)
    for block, rows, cols in blocks_of(sz):
        lanes = slice(block * LANES, (block + 1) * LANES)
        spread = select[block]
        high, middle, low = (
            jnp.dot(piece, spread, preferred_element_type=F32) for piece in pieces(grad[rows, cols])
        )
        picked = (low + middle) + high
        now = gens[:, lanes]
        gen_grad = costs[:1, lanes] + costs[1:, lanes] * now + dual[:, lanes] + (now - previous[:, lanes]) + picked
        now = jnp.minimum(jnp.maximum(now - 0.4 * gen_grad, 0.0), capacity[:, lanes])
        gens_out[:, lanes] = now
        if last:
            shed_out[:, block * sz.width : (block + 1) * sz.width] = shed_next[rows, cols]
            weighted_out[:1, lanes] = jnp.sum(weights[:, :1] * now, axis=0, keepdims=True)
            all_weights = jnp.sum(weights[:, :1], axis=0, keepdims=True)
            weighted_out[1:, lanes] = jnp.broadcast_to(all_weights, (7, LANES))
        else:
            inject[rows, cols] = (
                place(sz, now, select, block) + shed_next[rows, cols] - loads[rows, cols]
            ).astype(BF)


def add_kernel(first, second, out):
    out[...] = first[...] + second[...]


def finish_kernel(sz, *refs):
    parts = refs[: sz.chips]
    dual, gens, consensus, dual_out = refs[sz.chips :]
    total = parts[0][...]
    for part in parts[1:]:
        total = total + part[...]
    mean = total[:1] / total[1:2]
    consensus[...] = mean
    dual_out[...] = dual[...] + (gens[...] - mean)


def to_scen(n, away, value):
    return lax.ppermute(value, "scen", [(i, i ^ away) for i in range(n)])


def to_chip(n, away, value):
    return lax.ppermute(value, "line", [(i, i ^ (2 * away)) for i in range(n)])


def to_core(n, value):
    return lax.ppermute(value, "line", [(i, i ^ 1) for i in range(n)])


def local(
    mesh,
    shift_factors,
    gen_bus,
    commit,
    cost_coef,
    gen_cap,
    bus_loads,
    load_shed,
    dispatch,
    ph_dual,
    consensus_prev,
    scen_weight,
    flow_copy,
    flow_dual,
    balance_dual,
    flow_limit,
):
    lines, buses = shift_factors.shape
    rows, gens = dispatch.shape
    sz = Sizes(mesh, lines, buses, gens, rows)
    n_scen, n_line, chips = sz.scen, sz.line, sz.chips
    row = lambda v: v.reshape(1, -1)
    column = lambda v: jnp.broadcast_to(v[:, None], (rows, LANES))
    capacity, on, previous, limits = row(gen_cap), row(commit), row(consensus_prev), row(flow_limit)
    lam, weights = column(balance_dual), column(scen_weight)
    packed = (sz.fold * rows, sz.part)
    step_f = min(512, sz.half)
    step_b = next(s for s in (1024, 640, 512, 256, 128) if buses % s == 0)
    macs = sz.total * sz.chunk * buses

    generation, copies, duals = dispatch, flow_copy, flow_dual
    inject, shed, loads, select = call(
        functools.partial(start_kernel, sz),
        (dispatch, load_shed, bus_loads, row(gen_bus)),
        (
            (packed, BF),
            (packed, F32),
            (packed, F32),
            ((gens // LANES, sz.width, LANES), BF),
        ),
        limit=GRANT + lines * buses * 2,
    )
    for iteration in range(ITERS):
        own = [inject] + [to_chip(n_line, away, inject) for away in range(1, chips)]
        other = [to_core(n_line, value) for value in own]
        residuals, new_copies, new_duals = [], [], []
        final = iteration == ITERS - 1
        for chunk in range(CHUNKS):
            block = (2 * sz.pair, sz.half + (LANES if chunk == 0 else 0))
            flows = call(
                functools.partial(forward_kernel, sz, chunk, step_f),
                (*own, *other, shift_factors),
                [(block, F32)] + [(block, BF)] * (chips - 1),
                [((sz.total, buses), BF), ((chips, *block), F32)],
                flops=2 * macs,
                limit=GRANT - (nbytes(own + other) if iteration == 0 else 0),
            )
            parts = [flows[0]] + [to_scen(n_scen, away, flows[away]) for away in range(1, n_scen)]
            join = final and chunk == CHUNKS - 1 and CHUNKS > 1
            width = lines if join else sz.chunk
            whole = iteration == 0
            residual, copy_next, dual_next = call(
                functools.partial(residual_kernel, sz, chunk, join),
                (
                    *parts,
                    flow_copy if whole else copies[chunk],
                    flow_dual if whole else duals[chunk],
                    limits,
                    *((new_copies[0], new_duals[0]) if join else ()),
                ),
                [(block, BF), ((sz.pair, width), F32), ((sz.pair, width), F32)],
                keep=shift_factors,
            )
            new_copies.append(copy_next)
            new_duals.append(dual_next)
            residuals.append([residual] + [to_scen(n_scen, away, residual) for away in range(1, n_scen)])
        copies, duals = new_copies, new_duals
        before, balances = (), None
        for chunk in range(CHUNKS):
            last = chunk == CHUNKS - 1
            half = (sz.total // 2, buses)
            outs = [(half, F32), (half, BF)] if last else [((sz.total, buses), F32)]
            if chunk == 0:
                outs.append(((sz.pair, LANES), F32))
            found = call(
                functools.partial(backward_kernel, sz, chunk, step_b),
                (*residuals[chunk], shift_factors, *before),
                outs,
                [((sz.total, sz.chunk), BF)],
                flops=2 * macs,
            )
            if chunk == 0:
                balances = found[-1]
            before = found[:1]
        kept, sent = found[:2]
        sums = call(
            functools.partial(chip_kernel, sz),
            (kept, to_core(n_line, sent)),
            [(packed, F32)] + [(packed, BF)] * (chips - 1),
            [((chips, *packed), F32)],
            keep=None if final else shift_factors,
        )
        parts = [sums[0]] + [to_chip(n_line, away, sums[away]) for away in range(1, chips)]
        args = (*parts, balances, lam, shed, loads, generation, select, cost_coef, ph_dual, previous, capacity, on)
        if not final:
            generation, shed, lam, inject = call(
                functools.partial(update_kernel, sz, False),
                args,
                [((rows, gens), F32), (packed, F32), ((rows, LANES), F32), (packed, BF)],
                keep=shift_factors,
                limit=GRANT - nbytes((dispatch, shed, loads, select)),
            )
        else:
            generation, shed, lam, weighted = call(
                functools.partial(update_kernel, sz, True),
                (*args, weights),
                [((rows, gens), F32), ((rows, buses), F32), ((rows, LANES), F32), ((8, gens), F32)],
            )
    (weighted,) = call(add_kernel, (weighted, to_core(n_line, weighted)), [((8, gens), F32)])
    parts = [weighted] + [to_chip(n_line, away, weighted) for away in range(1, chips)]
    consensus, dual_out = call(
        functools.partial(finish_kernel, sz),
        (*parts, ph_dual, generation),
        [((1, gens), F32), ((rows, gens), F32)],
    )
    return generation, shed, copies[-1], duals[-1], lam[:, 0], consensus.reshape(-1), dual_out


def solution(mesh):
    return jax.shard_map(
        functools.partial(local, mesh),
        mesh=mesh,
        in_specs=(
            P("line", "scen"),
            P("scen"),
            P("scen"),
            P(None, "scen"),
            P("scen"),
            P("line", "scen"),
            P("line", "scen"),
            P("line", "scen"),
            P("line", "scen"),
            P("scen"),
            P("line"),
            P("scen", "line"),
            P("scen", "line"),
            P("line"),
            P("line"),
        ),
        out_specs=(
            P("line", "scen"),
            P("line", "scen"),
            P("scen", "line"),
            P("scen", "line"),
            P("line"),
            P("scen"),
            P("line", "scen"),
        ),
        check_vma=False,
    )
```

```python
import functools
import math

import jax
import jax.numpy as jnp
from jax import lax
from jax.experimental import pallas as pl
from jax.experimental.pallas import tpu as pltpu
from jax.sharding import PartitionSpec as P

BUSES = 20480
ITERS = 2
CHUNKS = 1
LANES = 128
GRANT = 11 << 20
BF = jnp.bfloat16
F32 = jnp.float32
WHOLE = pl.BlockSpec(memory_space=pltpu.VMEM)


def call(kernel, args, outs, scratch=(), flops=0, keep=None, limit=GRANT):
    size = sum(a.size * a.dtype.itemsize for a in args)
    if keep is not None:
        inner, args = kernel, (keep, *args)
        kernel = lambda kept, *refs: inner(*refs)
    return pl.pallas_call(
        kernel,
        in_specs=[WHOLE] * len(args),
        out_specs=[WHOLE] * len(outs),
        out_shape=[jax.ShapeDtypeStruct(shape, kind) for shape, kind in outs],
        scratch_shapes=[pltpu.VMEM(shape, kind) for shape, kind in scratch],
        compiler_params=pltpu.CompilerParams(vmem_limit_bytes=limit),
        cost_estimate=pl.CostEstimate(flops=flops, bytes_accessed=size, transcendentals=0),
    )(*args)


def nbytes(arrays):
    size = lambda a: math.prod(a.shape[:-2]) * -(-a.shape[-2] // 8) * 8 * a.shape[-1] * a.dtype.itemsize
    return sum(size(a) for a in arrays)


def pieces(value):
    high = value.astype(BF)
    rest = value - high.astype(F32)
    middle = rest.astype(BF)
    low = (rest - middle.astype(F32)).astype(BF)
    return high, middle, low


def dot_t(a, b):
    return lax.dot_general(a, b, (((1,), (1,)), ((), ())), preferred_element_type=F32)


class Sizes:
    def __init__(self, mesh, lines, buses, gens, rows):
        self.scen = mesh.shape["scen"]
        self.line = mesh.shape["line"]
        self.chips = self.line // 2
        assert self.chips == self.scen
        self.lines, self.buses, self.gens, self.rows = lines, buses, gens, rows
        self.pair = 2 * rows
        self.total = rows * self.line
        self.stretch = buses // gens
        self.width = self.stretch * LANES
        self.fold = next(f for f in (4, 2, 1) if buses % (f * self.width) == 0)
        self.part = buses // self.fold
        self.chunk = lines // CHUNKS
        self.half = self.chunk // 2


def where_am_i():
    line = lax.axis_index("line")
    return lax.axis_index("scen"), lax.div(line, 2), lax.rem(line, 2)


def place(sz, gens, select, block):
    spread = select[block]
    high, middle, low = pieces(gens)
    return (dot_t(low, spread) + dot_t(middle, spread)) + dot_t(high, spread)


def blocks_of(sz):
    per = sz.part // sz.width
    for block in range(sz.gens // LANES):
        fold, inner = divmod(block, per)
        yield block, slice(fold * sz.rows, (fold + 1) * sz.rows), slice(inner * sz.width, (inner + 1) * sz.width)


def start_kernel(sz, dispatch, shed, loads, gen_bus, inject, shed_p, loads_p, select):
    first = lax.axis_index("scen") * sz.buses
    bus = lax.broadcasted_iota(jnp.int32, (sz.width, LANES), 0)
    for block, rows, cols in blocks_of(sz):
        lanes = slice(block * LANES, (block + 1) * LANES)
        buses = slice(block * sz.width, (block + 1) * sz.width)
        local = gen_bus[:, lanes] - (first + block * sz.width)
        select[block] = (bus == local).astype(F32).astype(BF)
        here, load = shed[:, buses], loads[:, buses]
        inject[rows, cols] = (place(sz, dispatch[:, lanes], select, block) + here - load).astype(BF)
        shed_p[rows, cols] = here
        loads_p[rows, cols] = load


def forward_kernel(sz, chunk, step, *refs):
    chips = sz.chips
    own, other = refs[:chips], refs[chips : 2 * chips]
    factors = refs[2 * chips]
    outs = refs[2 * chips + 1 : 3 * chips + 1]
    inject, flows = refs[3 * chips + 1 :]
    scen, chip, core = where_am_i()
    extra = LANES if chunk == 0 else 0

    def gather(first, second):
        for slot in range(chips):
            for fold in range(sz.fold):
                rows = slice(fold * sz.rows, (fold + 1) * sz.rows)
                cols = slice(fold * sz.part, (fold + 1) * sz.part)
                base = slot * sz.pair
                inject[base : base + sz.rows, cols] = first[slot][rows, :]
                inject[base + sz.rows : base + sz.pair, cols] = second[slot][rows, :]

    @pl.when(core == 0)
    def _():
        gather(own, other)

    @pl.when(core == 1)
    def _():
        gather(other, own)

    if extra:
        total = jnp.sum(inject[...].astype(F32), axis=1, keepdims=True)
        high, middle, low = (piece.astype(F32) for piece in pieces(total))
        lane = lax.broadcasted_iota(jnp.int32, (sz.total, LANES), 1)
        tile = jnp.where(lane == 0, high, jnp.where(lane == 1, middle, jnp.where(lane == 2, low, 0.0)))
        for slot in range(chips):
            flows[slot, :, sz.half :] = jnp.zeros((2 * sz.pair, LANES), F32)
            flows[slot, : sz.pair, sz.half :] = tile[slot * sz.pair : (slot + 1) * sz.pair]
    for side in range(2):

        def body(i, _, side=side):
            source = pl.ds(pl.multiple_of(chunk * sz.chunk + side * sz.half + i * step, step), step)
            target = pl.ds(pl.multiple_of(i * step, step), step)
            product = dot_t(inject[...], factors[source, :])
            for slot in range(chips):
                flows[slot, side * sz.pair : (side + 1) * sz.pair, target] = product[
                    slot * sz.pair : (slot + 1) * sz.pair
                ]
            return 0

        lax.fori_loop(0, sz.half // step, body, 0)
    for away in range(chips):
        found = flows[chip ^ scen ^ away]
        outs[away][...] = found.astype(outs[away].dtype)


def residual_kernel(sz, chunk, join, *refs):
    scen = sz.scen
    parts = refs[:scen]
    copies, duals, limits = refs[scen : scen + 3]
    old = refs[scen + 3 : scen + 5] if join else None
    residual, copy_out, dual_out = refs[-3:]
    total = parts[0][...]
    for part in parts[1:]:
        total = total + part[...].astype(F32)
    for side in range(2):
        rows = slice(side * sz.pair, (side + 1) * sz.pair)
        start = chunk * sz.chunk + side * sz.half
        base = chunk * sz.chunk if copies.shape[1] == sz.lines else 0
        cols = slice(base + side * sz.half, base + (side + 1) * sz.half)
        to = slice(start, start + sz.half) if join else slice(side * sz.half, (side + 1) * sz.half)
        now, copy, dual = total[rows, : sz.half], copies[:, cols], duals[:, cols]
        limit = limits[:, start : start + sz.half]
        residual[rows, : sz.half] = (now - copy + dual).astype(BF)
        copy_next = jnp.minimum(jnp.maximum(now + dual, -limit), limit)
        copy_out[:, to] = copy_next
        dual_out[:, to] = dual + now - copy_next
    if join:
        copy_out[:, : chunk * sz.chunk] = old[0][...]
        dual_out[:, : chunk * sz.chunk] = old[1][...]
    if chunk == 0:
        balance = jnp.sum(total[:, sz.half :], axis=1, keepdims=True) / BUSES
        high, middle, low = (piece.astype(F32) for piece in pieces(balance))
        lane = lax.broadcasted_iota(jnp.int32, (2 * sz.pair, LANES), 1)
        tile = jnp.where(lane == 0, high, jnp.where(lane == 1, middle, jnp.where(lane == 2, low, 0.0)))
        residual[:, sz.half :] = tile.astype(BF)


def backward_kernel(sz, chunk, step, *refs):
    scen = sz.scen
    parts, factors = refs[:scen], refs[scen]
    before = refs[scen + 1] if chunk else None
    last = chunk == CHUNKS - 1
    residual = refs[-1]
    outs = refs[scen + 1 + (chunk > 0) : -1]
    me, chip, core = where_am_i()
    if chunk == 0:
        balances = outs[-1]
        for slot in range(scen):

            @pl.when(chip == (me ^ slot))
            def _(slot=slot):
                tile = parts[slot][: sz.pair, sz.half :].astype(F32)
                found = jnp.sum(tile, axis=1, keepdims=True)
                balances[...] = jnp.broadcast_to(found, (sz.pair, LANES))

    for slot in range(scen):
        for side in range(2):
            residual[slot * sz.pair : (slot + 1) * sz.pair, side * sz.half : (side + 1) * sz.half] = parts[slot][
                side * sz.pair : (side + 1) * sz.pair, : sz.half
            ]

    def body(i, _):
        cols = pl.ds(pl.multiple_of(i * step, step), step)
        product = jnp.dot(
            residual[...],
            factors[chunk * sz.chunk : (chunk + 1) * sz.chunk, cols],
            preferred_element_type=F32,
        )
        if chunk:
            product = before[:, cols] + product
        if not last:
            outs[0][:, cols] = product
            return 0
        kept, sent = outs[:2]
        even = [product[slot * sz.pair : slot * sz.pair + sz.rows] for slot in range(scen)]
        odd = [product[slot * sz.pair + sz.rows : (slot + 1) * sz.pair] for slot in range(scen)]
        even, odd = jnp.concatenate(even, 0), jnp.concatenate(odd, 0)
        kept[:, cols] = jnp.where(core == 0, even, odd)
        sent[:, cols] = jnp.where(core == 0, odd, even).astype(BF)
        return 0

    lax.fori_loop(0, sz.buses // step, body, 0)


def chip_kernel(sz, *refs):
    kept, received = refs[:2]
    outs, packed = refs[2:-1], refs[-1]
    scen, chip, core = where_am_i()
    total = kept[...] + received[...].astype(F32)
    for slot in range(sz.scen):
        for fold in range(sz.fold):
            packed[slot, fold * sz.rows : (fold + 1) * sz.rows, :] = total[
                slot * sz.rows : (slot + 1) * sz.rows, fold * sz.part : (fold + 1) * sz.part
            ]
    for away in range(sz.chips):
        found = packed[scen ^ chip ^ away]
        outs[away][...] = found.astype(outs[away].dtype)


def update_kernel(sz, last, *refs):
    parts = refs[: sz.chips]
    balances, lam, shed, loads, gens, select, costs, dual, previous, cap, commit = refs[sz.chips : sz.chips + 11]
    rest = refs[sz.chips + 11 :]
    core = where_am_i()[2]
    balance = jnp.where(core == 0, balances[: sz.rows, :1], balances[sz.rows :, :1])
    lam_now = lam[:, :1]
    shift = balance + lam_now
    shift = jnp.concatenate([shift] * sz.fold, 0)
    total = parts[0][...]
    for part in parts[1:]:
        total = total + part[...].astype(F32)
    grad = total + shift
    shed_next = jnp.minimum(jnp.maximum(shed[...] - 0.4 * (1.5 + grad), 0.0), loads[...])
    capacity = cap[...] * commit[...].astype(F32)
    if last:
        weights, gens_out, shed_out, lam_out, weighted_out = rest
    else:
        gens_out, shed_out, lam_out, inject = rest
        shed_out[...] = shed_next
    lam_out[...] = jnp.broadcast_to(lam_now + balance, lam_out.shape)
    for block, rows, cols in blocks_of(sz):
        lanes = slice(block * LANES, (block + 1) * LANES)
        spread = select[block]
        high, middle, low = (
            jnp.dot(piece, spread, preferred_element_type=F32) for piece in pieces(grad[rows, cols])
        )
        picked = (low + middle) + high
        now = gens[:, lanes]
        gen_grad = costs[:1, lanes] + costs[1:, lanes] * now + dual[:, lanes] + (now - previous[:, lanes]) + picked
        now = jnp.minimum(jnp.maximum(now - 0.4 * gen_grad, 0.0), capacity[:, lanes])
        gens_out[:, lanes] = now
        if last:
            shed_out[:, block * sz.width : (block + 1) * sz.width] = shed_next[rows, cols]
            weighted_out[:1, lanes] = jnp.sum(weights[:, :1] * now, axis=0, keepdims=True)
            all_weights = jnp.sum(weights[:, :1], axis=0, keepdims=True)
            weighted_out[1:, lanes] = jnp.broadcast_to(all_weights, (7, LANES))
        else:
            inject[rows, cols] = (
                place(sz, now, select, block) + shed_next[rows, cols] - loads[rows, cols]
            ).astype(BF)


def add_kernel(first, second, out):
    out[...] = first[...] + second[...]


def finish_kernel(sz, *refs):
    parts = refs[: sz.chips]
    dual, gens, consensus, dual_out = refs[sz.chips :]
    total = parts[0][...]
    for part in parts[1:]:
        total = total + part[...]
    mean = total[:1] / total[1:2]
    consensus[...] = mean
    dual_out[...] = dual[...] + (gens[...] - mean)


def to_scen(n, away, value):
    return lax.ppermute(value, "scen", [(i, i ^ away) for i in range(n)])


def to_chip(n, away, value):
    return lax.ppermute(value, "line", [(i, i ^ (2 * away)) for i in range(n)])


def to_core(n, value):
    return lax.ppermute(value, "line", [(i, i ^ 1) for i in range(n)])


def local(
    mesh,
    shift_factors,
    gen_bus,
    commit,
    cost_coef,
    gen_cap,
    bus_loads,
    load_shed,
    dispatch,
    ph_dual,
    consensus_prev,
    scen_weight,
    flow_copy,
    flow_dual,
    balance_dual,
    flow_limit,
):
    lines, buses = shift_factors.shape
    rows, gens = dispatch.shape
    sz = Sizes(mesh, lines, buses, gens, rows)
    n_scen, n_line, chips = sz.scen, sz.line, sz.chips
    row = lambda v: v.reshape(1, -1)
    column = lambda v: jnp.broadcast_to(v[:, None], (rows, LANES))
    capacity, on, previous, limits = row(gen_cap), row(commit), row(consensus_prev), row(flow_limit)
    lam, weights = column(balance_dual), column(scen_weight)
    packed = (sz.fold * rows, sz.part)
    step_f = min(512, sz.half)
    step_b = next(s for s in (1024, 640, 512, 256, 128) if buses % s == 0)
    macs = sz.total * sz.chunk * buses

    generation, copies, duals = dispatch, flow_copy, flow_dual
    first = (dispatch, load_shed, bus_loads, row(gen_bus))
    made = ((packed, BF), (packed, F32), (packed, F32), ((gens // LANES, sz.width, LANES), BF))
    inject, shed, loads, select = call(
        functools.partial(start_kernel, sz),
        first,
        made,
        flops=1000 * lines * buses,
        limit=GRANT - nbytes(first + tuple(jax.ShapeDtypeStruct(*each) for each in made)) - (1 << 16),
    )
    for iteration in range(ITERS):
        own = [inject] + [to_chip(n_line, away, inject) for away in range(1, chips)]
        other = [to_core(n_line, value) for value in own]
        residuals, new_copies, new_duals = [], [], []
        final = iteration == ITERS - 1
        for chunk in range(CHUNKS):
            block = (2 * sz.pair, sz.half + (LANES if chunk == 0 else 0))
            flows = call(
                functools.partial(forward_kernel, sz, chunk, step_f),
                (*own, *other, shift_factors),
                [(block, F32)] + [(block, BF)] * (chips - 1),
                [((sz.total, buses), BF), ((chips, *block), F32)],
                flops=2 * macs,
                limit=GRANT - (nbytes(own + other) if iteration == 0 else 0),
            )
            parts = [flows[0]] + [to_scen(n_scen, away, flows[away]) for away in range(1, n_scen)]
            join = final and chunk == CHUNKS - 1 and CHUNKS > 1
            width = lines if join else sz.chunk
            whole = iteration == 0
            residual, copy_next, dual_next = call(
                functools.partial(residual_kernel, sz, chunk, join),
                (
                    *parts,
                    flow_copy if whole else copies[chunk],
                    flow_dual if whole else duals[chunk],
                    limits,
                    *((new_copies[0], new_duals[0]) if join else ()),
                ),
                [(block, BF), ((sz.pair, width), F32), ((sz.pair, width), F32)],
                keep=shift_factors,
            )
            new_copies.append(copy_next)
            new_duals.append(dual_next)
            residuals.append([residual] + [to_scen(n_scen, away, residual) for away in range(1, n_scen)])
        copies, duals = new_copies, new_duals
        before, balances = (), None
        for chunk in range(CHUNKS):
            last = chunk == CHUNKS - 1
            half = (sz.total // 2, buses)
            outs = [(half, F32), (half, BF)] if last else [((sz.total, buses), F32)]
            if chunk == 0:
                outs.append(((sz.pair, LANES), F32))
            found = call(
                functools.partial(backward_kernel, sz, chunk, step_b),
                (*residuals[chunk], shift_factors, *before),
                outs,
                [((sz.total, sz.chunk), BF)],
                flops=2 * macs,
            )
            if chunk == 0:
                balances = found[-1]
            before = found[:1]
        kept, sent = found[:2]
        sums = call(
            functools.partial(chip_kernel, sz),
            (kept, to_core(n_line, sent)),
            [(packed, F32)] + [(packed, BF)] * (chips - 1),
            [((chips, *packed), F32)],
            keep=None if final else shift_factors,
        )
        parts = [sums[0]] + [to_chip(n_line, away, sums[away]) for away in range(1, chips)]
        args = (*parts, balances, lam, shed, loads, generation, select, cost_coef, ph_dual, previous, capacity, on)
        if not final:
            generation, shed, lam, inject = call(
                functools.partial(update_kernel, sz, False),
                args,
                [((rows, gens), F32), (packed, F32), ((rows, LANES), F32), (packed, BF)],
                keep=shift_factors,
                limit=GRANT - nbytes((dispatch, shed, loads, select)),
            )
        else:
            generation, shed, lam, weighted = call(
                functools.partial(update_kernel, sz, True),
                (*args, weights),
                [((rows, gens), F32), ((rows, buses), F32), ((rows, LANES), F32), ((8, gens), F32)],
            )
    (weighted,) = call(add_kernel, (weighted, to_core(n_line, weighted)), [((8, gens), F32)])
    parts = [weighted] + [to_chip(n_line, away, weighted) for away in range(1, chips)]
    consensus, dual_out = call(
        functools.partial(finish_kernel, sz),
        (*parts, ph_dual, generation),
        [((1, gens), F32), ((rows, gens), F32)],
    )
    return generation, shed, copies[-1], duals[-1], lam[:, 0], consensus.reshape(-1), dual_out


def solution(mesh):
    return jax.shard_map(
        functools.partial(local, mesh),
        mesh=mesh,
        in_specs=(
            P("line", "scen"),
            P("scen"),
            P("scen"),
            P(None, "scen"),
            P("scen"),
            P("line", "scen"),
            P("line", "scen"),
            P("line", "scen"),
            P("line", "scen"),
            P("scen"),
            P("line"),
            P("scen", "line"),
            P("scen", "line"),
            P("line"),
            P("line"),
        ),
        out_specs=(
            P("line", "scen"),
            P("line", "scen"),
            P("scen", "line"),
            P("scen", "line"),
            P("line"),
            P("scen"),
            P("line", "scen"),
        ),
        check_vma=False,
    )
```

```python
import functools
import math

import jax
import jax.numpy as jnp
from jax import lax
from jax.experimental import pallas as pl
from jax.experimental.pallas import tpu as pltpu
from jax.sharding import PartitionSpec as P

BUSES = 20480
ITERS = 2
CHUNKS = 2
LANES = 128
GRANT = 11 << 20
BF = jnp.bfloat16
F32 = jnp.float32
WHOLE = pl.BlockSpec(memory_space=pltpu.VMEM)


def call(kernel, args, outs, scratch=(), flops=0, keep=None, limit=GRANT):
    size = sum(a.size * a.dtype.itemsize for a in args)
    if keep is not None:
        inner, args = kernel, (keep, *args)
        kernel = lambda kept, *refs: inner(*refs)
    return pl.pallas_call(
        kernel,
        in_specs=[WHOLE] * len(args),
        out_specs=[WHOLE] * len(outs),
        out_shape=[jax.ShapeDtypeStruct(shape, kind) for shape, kind in outs],
        scratch_shapes=[pltpu.VMEM(shape, kind) for shape, kind in scratch],
        compiler_params=pltpu.CompilerParams(vmem_limit_bytes=limit),
        cost_estimate=pl.CostEstimate(flops=flops, bytes_accessed=size, transcendentals=0),
    )(*args)


def nbytes(arrays):
    size = lambda a: math.prod(a.shape[:-2]) * -(-a.shape[-2] // 8) * 8 * a.shape[-1] * a.dtype.itemsize
    return sum(size(a) for a in arrays)


def pieces(value):
    high = value.astype(BF)
    rest = value - high.astype(F32)
    middle = rest.astype(BF)
    low = (rest - middle.astype(F32)).astype(BF)
    return high, middle, low


def stacked(value):
    rows, columns = value.shape
    below = [jnp.zeros((8 - rows, columns), F32)] if rows < 8 else []
    parts = []
    for piece in pieces(value):
        parts += [piece.astype(F32)] + below
    return jnp.concatenate(parts, 0).astype(BF)


def unstacked(product, rows):
    return (product[16 : 16 + rows] + product[8 : 8 + rows]) + product[:rows]


def dot_t(a, b):
    return lax.dot_general(a, b, (((1,), (1,)), ((), ())), preferred_element_type=F32)


class Sizes:
    def __init__(self, mesh, lines, buses, gens, rows):
        self.scen = mesh.shape["scen"]
        self.line = mesh.shape["line"]
        self.chips = self.line // 2
        assert self.chips == self.scen
        self.lines, self.buses, self.gens, self.rows = lines, buses, gens, rows
        self.pair = 2 * rows
        self.total = rows * self.line
        self.stretch = buses // gens
        self.width = self.stretch * LANES
        self.fold = next(f for f in (4, 2, 1) if buses % (f * self.width) == 0)
        self.part = buses // self.fold
        self.chunk = lines // CHUNKS
        self.half = self.chunk // 2


def where_am_i():
    line = lax.axis_index("line")
    return lax.axis_index("scen"), lax.div(line, 2), lax.rem(line, 2)


def place(sz, gens, select, block):
    return unstacked(dot_t(stacked(gens), select[block]), sz.rows)


def blocks_of(sz):
    per = sz.part // sz.width
    for block in range(sz.gens // LANES):
        fold, inner = divmod(block, per)
        yield block, slice(fold * sz.rows, (fold + 1) * sz.rows), slice(inner * sz.width, (inner + 1) * sz.width)


def start_kernel(sz, dispatch, shed, loads, gen_bus, inject, shed_p, loads_p, select):
    first = lax.axis_index("scen") * sz.buses
    bus = lax.broadcasted_iota(jnp.int32, (sz.width, LANES), 0)
    for block, rows, cols in blocks_of(sz):
        lanes = slice(block * LANES, (block + 1) * LANES)
        buses = slice(block * sz.width, (block + 1) * sz.width)
        local = gen_bus[:, lanes] - (first + block * sz.width)
        select[block] = (bus == local).astype(F32).astype(BF)
        served, load = shed[:, buses], loads[:, buses]
        inject[rows, cols] = (place(sz, dispatch[:, lanes], select, block) + served - load).astype(BF)
        shed_p[rows, cols] = served
        loads_p[rows, cols] = load


def forward_kernel(sz, chunk, step, *refs):
    chips = sz.chips
    own, other = refs[:chips], refs[chips : 2 * chips]
    factors = refs[2 * chips]
    outs = refs[2 * chips + 1 : 3 * chips + 1]
    inject, flows = refs[3 * chips + 1 :]
    scen, chip, core = where_am_i()
    extra = LANES if chunk == 0 else 0

    def gather(first, second):
        for slot in range(chips):
            for fold in range(sz.fold):
                rows = slice(fold * sz.rows, (fold + 1) * sz.rows)
                cols = slice(fold * sz.part, (fold + 1) * sz.part)
                base = slot * sz.pair
                inject[base : base + sz.rows, cols] = first[slot][rows, :]
                inject[base + sz.rows : base + sz.pair, cols] = second[slot][rows, :]

    @pl.when(core == 0)
    def _():
        gather(own, other)

    @pl.when(core == 1)
    def _():
        gather(other, own)

    if extra:
        total = jnp.sum(inject[...].astype(F32), axis=1, keepdims=True)
        high, middle, low = (piece.astype(F32) for piece in pieces(total))
        lane = lax.broadcasted_iota(jnp.int32, (sz.total, LANES), 1)
        tile = jnp.where(lane == 0, high, jnp.where(lane == 1, middle, jnp.where(lane == 2, low, 0.0)))
        for slot in range(chips):
            flows[slot, :, sz.half :] = jnp.zeros((2 * sz.pair, LANES), F32)
            flows[slot, : sz.pair, sz.half :] = tile[slot * sz.pair : (slot + 1) * sz.pair]
    for side in range(2):

        def body(i, _, side=side):
            source = pl.ds(pl.multiple_of(chunk * sz.chunk + side * sz.half + i * step, step), step)
            target = pl.ds(pl.multiple_of(i * step, step), step)
            product = dot_t(factors[source, :], inject[...]).T
            for slot in range(chips):
                flows[slot, side * sz.pair : (side + 1) * sz.pair, target] = product[
                    slot * sz.pair : (slot + 1) * sz.pair
                ]
            return 0

        lax.fori_loop(0, sz.half // step, body, 0)
    for away in range(chips):
        found = flows[chip ^ scen ^ away]
        outs[away][...] = found.astype(outs[away].dtype)


def residual_kernel(sz, chunk, join, *refs):
    scen = sz.scen
    parts = refs[:scen]
    copies, duals, limits = refs[scen : scen + 3]
    wide = sz.half + LANES
    if chunk == 0:
        flows = refs[scen + 3 : 2 * scen + 2]
        residual, copy_out, dual_out = refs[2 * scen + 2 : 2 * scen + 5]
        messages = refs[2 * scen + 5 :]
    else:
        old = refs[scen + 3 : scen + 5] if join else None
        residual, copy_out, dual_out = refs[-3:]
    total = parts[0][...]
    for part in parts[1:]:
        total = total + part[:, wide if chunk else 0 :].astype(F32)
    for side in range(2):
        rows = slice(side * sz.pair, (side + 1) * sz.pair)
        start = chunk * sz.chunk + side * sz.half
        base = chunk * sz.chunk if copies.shape[1] == sz.lines else 0
        cols = slice(base + side * sz.half, base + (side + 1) * sz.half)
        to = slice(start, start + sz.half) if join else slice(side * sz.half, (side + 1) * sz.half)
        now, copy, dual = total[rows, : sz.half], copies[:, cols], duals[:, cols]
        limit = limits[:, start : start + sz.half]
        residual[rows, : sz.half] = (now - copy + dual).astype(BF)
        copy_next = jnp.minimum(jnp.maximum(now + dual, -limit), limit)
        copy_out[:, to] = copy_next
        dual_out[:, to] = dual + now - copy_next
    if chunk == 0:
        balance = jnp.sum(total[:, sz.half :], axis=1, keepdims=True) / BUSES
        high, middle, low = (piece.astype(F32) for piece in pieces(balance))
        lane = lax.broadcasted_iota(jnp.int32, (2 * sz.pair, LANES), 1)
        tile = jnp.where(lane == 0, high, jnp.where(lane == 1, middle, jnp.where(lane == 2, low, 0.0)))
        residual[:, sz.half :] = tile.astype(BF)
        for message, flow in zip(messages, flows):
            message[:, :wide] = residual[...]
            message[:, wide:] = flow[...]
    elif join:
        copy_out[:, : chunk * sz.chunk] = old[0][...]
        dual_out[:, : chunk * sz.chunk] = old[1][...]


def backward_kernel(sz, chunk, step, *refs):
    scen = sz.scen
    parts, factors = refs[:scen], refs[scen]
    before = refs[scen + 1] if chunk else None
    last = chunk == CHUNKS - 1
    residual = refs[-1]
    outs = refs[scen + 1 + (chunk > 0) : -1]
    me, chip, core = where_am_i()
    if chunk == 0:
        balances = outs[-1]
        for slot in range(scen):

            @pl.when(chip == (me ^ slot))
            def _(slot=slot):
                tile = parts[slot][: sz.pair, sz.half : sz.half + LANES].astype(F32)
                found = jnp.sum(tile, axis=1, keepdims=True)
                balances[...] = jnp.broadcast_to(found, (sz.pair, LANES))

    for slot in range(scen):
        for side in range(2):
            residual[slot * sz.pair : (slot + 1) * sz.pair, side * sz.half : (side + 1) * sz.half] = parts[slot][
                side * sz.pair : (side + 1) * sz.pair, : sz.half
            ]

    def body(i, _):
        cols = pl.ds(pl.multiple_of(i * step, step), step)
        product = jnp.dot(
            residual[...],
            factors[chunk * sz.chunk : (chunk + 1) * sz.chunk, cols],
            preferred_element_type=F32,
        )
        if chunk:
            product = before[:, cols] + product
        if not last:
            outs[0][:, cols] = product
            return 0
        kept, sent = outs[:2]
        even = [product[slot * sz.pair : slot * sz.pair + sz.rows] for slot in range(scen)]
        odd = [product[slot * sz.pair + sz.rows : (slot + 1) * sz.pair] for slot in range(scen)]
        even, odd = jnp.concatenate(even, 0), jnp.concatenate(odd, 0)
        kept[:, cols] = jnp.where(core == 0, even, odd)
        sent[:, cols] = jnp.where(core == 0, odd, even).astype(BF)
        return 0

    lax.fori_loop(0, sz.buses // step, body, 0)


def chip_kernel(sz, *refs):
    kept, received = refs[:2]
    outs, packed = refs[2:-1], refs[-1]
    scen, chip, core = where_am_i()
    total = kept[...] + received[...].astype(F32)
    for slot in range(sz.scen):
        for fold in range(sz.fold):
            packed[slot, fold * sz.rows : (fold + 1) * sz.rows, :] = total[
                slot * sz.rows : (slot + 1) * sz.rows, fold * sz.part : (fold + 1) * sz.part
            ]
    for away in range(sz.chips):
        found = packed[scen ^ chip ^ away]
        outs[away][...] = found.astype(outs[away].dtype)


def update_kernel(sz, last, *refs):
    parts = refs[: sz.chips]
    balances, lam, shed, loads, gens, select, costs, dual, previous, cap, commit = refs[sz.chips : sz.chips + 11]
    rest = refs[sz.chips + 11 :]
    core = where_am_i()[2]
    balance = jnp.where(core == 0, balances[: sz.rows, :1], balances[sz.rows :, :1])
    lam_now = lam[:, :1]
    shift = balance + lam_now
    shift = jnp.concatenate([shift] * sz.fold, 0)
    total = parts[0][...]
    for part in parts[1:]:
        total = total + part[...].astype(F32)
    grad = total + shift
    shed_next = jnp.minimum(jnp.maximum(shed[...] - 0.4 * (1.5 + grad), 0.0), loads[...])
    capacity = cap[...] * commit[...].astype(F32)
    if last:
        weights, gens_out, shed_out, lam_out, weighted_out, dual_out = rest
    else:
        gens_out, shed_out, lam_out, inject = rest
        shed_out[...] = shed_next
    lam_out[...] = jnp.broadcast_to(lam_now + balance, lam_out.shape)
    for block, rows, cols in blocks_of(sz):
        lanes = slice(block * LANES, (block + 1) * LANES)
        picked = jnp.dot(stacked(grad[rows, cols]), select[block], preferred_element_type=F32)
        picked = unstacked(picked, sz.rows)
        now = gens[:, lanes]
        gen_grad = costs[:1, lanes] + costs[1:, lanes] * now + dual[:, lanes] + (now - previous[:, lanes]) + picked
        now = jnp.minimum(jnp.maximum(now - 0.4 * gen_grad, 0.0), capacity[:, lanes])
        gens_out[:, lanes] = now
        if last:
            dual_out[:, lanes] = dual[:, lanes] + now
            shed_out[:, block * sz.width : (block + 1) * sz.width] = shed_next[rows, cols]
            weighted_out[:1, lanes] = jnp.sum(weights[:, :1] * now, axis=0, keepdims=True)
            all_weights = jnp.sum(weights[:, :1], axis=0, keepdims=True)
            weighted_out[1:, lanes] = jnp.broadcast_to(all_weights, (7, LANES))
        else:
            inject[rows, cols] = (
                place(sz, now, select, block) + shed_next[rows, cols] - loads[rows, cols]
            ).astype(BF)


def add_kernel(first, second, out):
    out[...] = first[...] + second[...]


def finish_kernel(sz, *refs):
    parts = refs[: sz.chips]
    dual, consensus, dual_out = refs[sz.chips :]
    total = parts[0][...]
    for part in parts[1:]:
        total = total + part[...]
    mean = total[:1] / total[1:2]
    consensus[...] = mean
    dual_out[...] = dual[...] - mean


def to_scen(n, away, value):
    return lax.ppermute(value, "scen", [(i, i ^ away) for i in range(n)])


def to_chip(n, away, value):
    return lax.ppermute(value, "line", [(i, i ^ (2 * away)) for i in range(n)])


def to_core(n, value):
    return lax.ppermute(value, "line", [(i, i ^ 1) for i in range(n)])


def local(
    mesh,
    shift_factors,
    gen_bus,
    commit,
    cost_coef,
    gen_cap,
    bus_loads,
    load_shed,
    dispatch,
    ph_dual,
    consensus_prev,
    scen_weight,
    flow_copy,
    flow_dual,
    balance_dual,
    flow_limit,
):
    lines, buses = shift_factors.shape
    rows, gens = dispatch.shape
    sz = Sizes(mesh, lines, buses, gens, rows)
    n_scen, n_line, chips = sz.scen, sz.line, sz.chips
    row = lambda v: v.reshape(1, -1)
    column = lambda v: jnp.broadcast_to(v[:, None], (rows, LANES))
    capacity, on, previous, limits = row(gen_cap), row(commit), row(consensus_prev), row(flow_limit)
    lam, weights = column(balance_dual), column(scen_weight)
    packed = (sz.fold * rows, sz.part)
    step_f = min(1024, sz.half)
    step_b = next(s for s in (1024, 640, 512, 256, 128) if buses % s == 0)
    macs = sz.total * sz.chunk * buses

    generation, copies, duals = dispatch, flow_copy, flow_dual
    first = (dispatch, load_shed, bus_loads, row(gen_bus))
    made = ((packed, BF), (packed, F32), (packed, F32), ((gens // LANES, sz.width, LANES), BF))
    inject, shed, loads, select = call(
        functools.partial(start_kernel, sz),
        first,
        made,
        flops=1000 * lines * buses,
        limit=GRANT - nbytes(first + tuple(jax.ShapeDtypeStruct(*each) for each in made)) - (1 << 16),
    )
    for iteration in range(ITERS):
        own = [inject] + [to_chip(n_line, away, inject) for away in range(1, chips)]
        other = [to_core(n_line, value) for value in own]
        final = iteration == ITERS - 1
        tall = 2 * sz.pair
        widths = (sz.half + LANES, sz.half)
        flows = []
        for chunk in range(CHUNKS):
            block = (tall, widths[chunk])
            flows.append(
                call(
                    functools.partial(forward_kernel, sz, chunk, step_f),
                    (*own, *other, shift_factors),
                    [(block, F32)] + [(block, BF)] * (n_scen - 1),
                    [((sz.total, buses), BF), ((chips, *block), F32)],
                    flops=2 * macs,
                    limit=GRANT - (nbytes(own + other) if iteration == 0 else 0),
                )
            )
            if chunk == 0:
                parts = [flows[0][0]] + [to_scen(n_scen, away, flows[0][away]) for away in range(1, n_scen)]
        state = lambda width: [((sz.pair, width), F32)] * 2
        old = (flow_copy, flow_dual) if iteration == 0 else None
        first_res, first_copy, first_dual, *messages = call(
            functools.partial(residual_kernel, sz, 0, False),
            (*parts, *(old or (copies[0], duals[0])), limits, *flows[1][1:]),
            [((tall, widths[0]), BF), *state(sz.chunk)] + [((tall, sum(widths)), BF)] * (n_scen - 1),
            keep=shift_factors,
        )
        got = [to_scen(n_scen, away, message) for away, message in enumerate(messages, 1)]
        second_res, second_copy, second_dual = call(
            functools.partial(residual_kernel, sz, 1, final),
            (
                flows[1][0],
                *got,
                *(old or (copies[1], duals[1])),
                limits,
                *((first_copy, first_dual) if final else ()),
            ),
            [((tall, widths[1]), BF), *state(lines if final else sz.chunk)],
            keep=shift_factors,
        )
        residuals = [
            [first_res, *got],
            [second_res] + [to_scen(n_scen, away, second_res) for away in range(1, n_scen)],
        ]
        new_copies, new_duals = [first_copy, second_copy], [first_dual, second_dual]
        copies, duals = new_copies, new_duals
        before, balances = (), None
        for chunk in range(CHUNKS):
            last = chunk == CHUNKS - 1
            half = (sz.total // 2, buses)
            outs = [(half, F32), (half, BF)] if last else [((sz.total, buses), F32)]
            if chunk == 0:
                outs.append(((sz.pair, LANES), F32))
            found = call(
                functools.partial(backward_kernel, sz, chunk, step_b),
                (*residuals[chunk], shift_factors, *before),
                outs,
                [((sz.total, sz.chunk), BF)],
                flops=2 * macs,
            )
            if chunk == 0:
                balances = found[-1]
            before = found[:1]
        kept, sent = found[:2]
        sums = call(
            functools.partial(chip_kernel, sz),
            (kept, to_core(n_line, sent)),
            [(packed, F32)] + [(packed, BF)] * (chips - 1),
            [((chips, *packed), F32)],
            keep=None if final else shift_factors,
        )
        parts = [sums[0]] + [to_chip(n_line, away, sums[away]) for away in range(1, chips)]
        args = (*parts, balances, lam, shed, loads, generation, select, cost_coef, ph_dual, previous, capacity, on)
        if not final:
            generation, shed, lam, inject = call(
                functools.partial(update_kernel, sz, False),
                args,
                [((rows, gens), F32), (packed, F32), ((rows, LANES), F32), (packed, BF)],
                keep=shift_factors,
                limit=GRANT - nbytes((dispatch, shed, loads, select)),
            )
        else:
            generation, shed, lam, weighted, dual_sum = call(
                functools.partial(update_kernel, sz, True),
                (*args, weights),
                [((rows, gens), F32), ((rows, buses), F32), ((rows, LANES), F32), ((8, gens), F32), ((rows, gens), F32)],
            )
    (weighted,) = call(add_kernel, (weighted, to_core(n_line, weighted)), [((8, gens), F32)])
    parts = [weighted] + [to_chip(n_line, away, weighted) for away in range(1, chips)]
    consensus, dual_out = call(
        functools.partial(finish_kernel, sz),
        (*parts, dual_sum),
        [((1, gens), F32), ((rows, gens), F32)],
    )
    return generation, shed, copies[-1], duals[-1], lam[:, 0], consensus.reshape(-1), dual_out


def solution(mesh):
    return jax.shard_map(
        functools.partial(local, mesh),
        mesh=mesh,
        in_specs=(
            P("line", "scen"),
            P("scen"),
            P("scen"),
            P(None, "scen"),
            P("scen"),
            P("line", "scen"),
            P("line", "scen"),
            P("line", "scen"),
            P("line", "scen"),
            P("scen"),
            P("line"),
            P("scen", "line"),
            P("scen", "line"),
            P("line"),
            P("line"),
        ),
        out_specs=(
            P("line", "scen"),
            P("line", "scen"),
            P("scen", "line"),
            P("scen", "line"),
            P("line"),
            P("scen"),
            P("line", "scen"),
        ),
        check_vma=False,
    )
```

```python
import functools
import math

import jax
import jax.numpy as jnp
from jax import lax
from jax.experimental import pallas as pl
from jax.experimental.pallas import tpu as pltpu
from jax.sharding import PartitionSpec as P

BUSES = 20480
ITERS = 2
CHUNKS = 2
FIRST_SHARE = 0.5625
EARLY_SHARE = 0.4375
LANES = 128
GRANT = 11 << 20
BF = jnp.bfloat16
F32 = jnp.float32
WHOLE = pl.BlockSpec(memory_space=pltpu.VMEM)


def call(kernel, args, outs, scratch=(), flops=0, keep=None, limit=GRANT):
    size = sum(a.size * a.dtype.itemsize for a in args)
    if keep is not None:
        inner, args = kernel, (keep, *args)
        kernel = lambda kept, *refs: inner(*refs)
    return pl.pallas_call(
        kernel,
        in_specs=[WHOLE] * len(args),
        out_specs=[WHOLE] * len(outs),
        out_shape=[jax.ShapeDtypeStruct(shape, kind) for shape, kind in outs],
        scratch_shapes=[pltpu.VMEM(shape, kind) for shape, kind in scratch],
        compiler_params=pltpu.CompilerParams(vmem_limit_bytes=limit),
        cost_estimate=pl.CostEstimate(flops=flops, bytes_accessed=size, transcendentals=0),
    )(*args)


def nbytes(arrays):
    size = lambda a: math.prod(a.shape[:-2]) * -(-a.shape[-2] // 8) * 8 * a.shape[-1] * a.dtype.itemsize
    return sum(size(a) for a in arrays)


def pieces(value):
    high = value.astype(BF)
    rest = value - high.astype(F32)
    middle = rest.astype(BF)
    low = (rest - middle.astype(F32)).astype(BF)
    return high, middle, low


def stacked(value):
    rows, columns = value.shape
    below = [jnp.zeros((8 - rows, columns), F32)] if rows < 8 else []
    parts = []
    for piece in pieces(value):
        parts += [piece.astype(F32)] + below
    return jnp.concatenate(parts, 0).astype(BF)


def unstacked(product, rows):
    return (product[16 : 16 + rows] + product[8 : 8 + rows]) + product[:rows]


def dot_t(a, b):
    return lax.dot_general(a, b, (((1,), (1,)), ((), ())), preferred_element_type=F32)


class Sizes:
    def __init__(self, mesh, lines, buses, gens, rows):
        self.scen = mesh.shape["scen"]
        self.line = mesh.shape["line"]
        self.chips = self.line // 2
        assert self.chips == self.scen
        self.lines, self.buses, self.gens, self.rows = lines, buses, gens, rows
        self.pair = 2 * rows
        self.total = rows * self.line
        self.stretch = buses // gens
        self.width = self.stretch * LANES
        self.fold = next(f for f in (4, 2, 1) if buses % (f * self.width) == 0)
        self.part = buses // self.fold
        tiles = lambda share, least, most: min(max(round(share * lines / 2 / LANES), least), most) * LANES
        first = tiles(FIRST_SHARE, 2, lines // 2 // LANES - 1)
        self.halves = (first, lines // 2 - first)
        self.early = tiles(EARLY_SHARE, 1, first // LANES - 1)
        self.starts = (0, 2 * first)
        self.ranges = (((0, self.early), (first, first + self.early)), ((self.early, first), (first + self.early, lines)))


def where_am_i():
    line = lax.axis_index("line")
    return lax.axis_index("scen"), lax.div(line, 2), lax.rem(line, 2)


def place(sz, gens, select, block):
    return unstacked(dot_t(stacked(gens), select[block]), sz.rows)


def blocks_of(sz):
    per = sz.part // sz.width
    for block in range(sz.gens // LANES):
        fold, inner = divmod(block, per)
        yield block, slice(fold * sz.rows, (fold + 1) * sz.rows), slice(inner * sz.width, (inner + 1) * sz.width)


def start_kernel(sz, dispatch, net, gen_bus, inject, select):
    first = lax.axis_index("scen") * sz.buses
    bus = lax.broadcasted_iota(jnp.int32, (sz.width, LANES), 0)
    for block, rows, cols in blocks_of(sz):
        lanes = slice(block * LANES, (block + 1) * LANES)
        buses = slice(block * sz.width, (block + 1) * sz.width)
        local = gen_bus[:, lanes] - (first + block * sz.width)
        select[block] = (bus == local).astype(F32).astype(BF)
        inject[rows, cols] = (place(sz, dispatch[:, lanes], select, block) + net[:, buses]).astype(BF)


def forward_kernel(sz, chunk, *refs):
    chips = sz.chips
    own, other = refs[:chips], refs[chips : 2 * chips]
    factors = refs[2 * chips]
    outs = refs[2 * chips + 1 : 3 * chips + 1]
    inject, flows = refs[3 * chips + 1 :]
    scen, chip, core = where_am_i()
    half = sz.halves[chunk]

    def gather(first, second):
        for slot in range(chips):
            for fold in range(sz.fold):
                rows = slice(fold * sz.rows, (fold + 1) * sz.rows)
                cols = slice(fold * sz.part, (fold + 1) * sz.part)
                base = slot * sz.pair
                inject[base : base + sz.rows, cols] = first[slot][rows, :]
                inject[base + sz.rows : base + sz.pair, cols] = second[slot][rows, :]

    @pl.when(core == 0)
    def _():
        gather(own, other)

    @pl.when(core == 1)
    def _():
        gather(other, own)

    if chunk == 0:
        total = jnp.sum(inject[...].astype(F32), axis=1, keepdims=True)
        high, middle, low = (piece.astype(F32) for piece in pieces(total))
        lane = lax.broadcasted_iota(jnp.int32, (sz.total, LANES), 1)
        tile = jnp.where(lane == 0, high, jnp.where(lane == 1, middle, jnp.where(lane == 2, low, 0.0)))
        for slot in range(chips):
            flows[slot, :, half:] = jnp.zeros((2 * sz.pair, LANES), F32)
            flows[slot, : sz.pair, half:] = tile[slot * sz.pair : (slot + 1) * sz.pair]
    for side in range(2):
        start = sz.starts[chunk] + side * half
        product = dot_t(factors[start : start + half, :], inject[...]).T
        for slot in range(chips):
            flows[slot, side * sz.pair : (side + 1) * sz.pair, :half] = product[slot * sz.pair : (slot + 1) * sz.pair]
    for away in range(chips):
        found = flows[chip ^ scen ^ away]
        outs[away][...] = found.astype(outs[away].dtype)


def residual_kernel(sz, chunk, *refs):
    scen = sz.scen
    half, early, start = sz.halves[chunk], sz.early, sz.starts[chunk]
    parts = refs[:scen]
    copies, duals, limits = refs[scen : scen + 3]
    if chunk == 0:
        flows = refs[scen + 3 : 2 * scen + 2]
        residual, rest, copy_out, dual_out = refs[2 * scen + 2 : 2 * scen + 6]
        messages = refs[2 * scen + 6 :]
        skip = 0
    else:
        rest, residual, copy_out, dual_out = refs[scen + 3 :]
        before = rest.shape[1]
        residual[:, :before] = rest[...]
        skip = early + LANES
    total = parts[0][...]
    for part in parts[1:]:
        total = total + part[:, skip:].astype(F32)
    for side in range(2):
        rows = slice(side * sz.pair, (side + 1) * sz.pair)
        base = start if copies.shape[1] == sz.lines else 0
        cols = slice(base + side * half, base + (side + 1) * half)
        to = slice(side * half, (side + 1) * half)
        now, copy, dual = total[rows, :half], copies[:, cols], duals[:, cols]
        limit = limits[:, start + side * half : start + (side + 1) * half]
        found = (now - copy + dual).astype(BF)
        if chunk == 0:
            residual[rows, :early] = found[:, :early]
            rest[rows, :] = found[:, early:]
        else:
            residual[rows, before:] = found
        copy_next = jnp.minimum(jnp.maximum(now + dual, -limit), limit)
        copy_out[:, to] = copy_next
        dual_out[:, to] = dual + now - copy_next
    if chunk == 0:
        balance = jnp.sum(total[:, half:], axis=1, keepdims=True) / BUSES
        high, middle, low = (piece.astype(F32) for piece in pieces(balance))
        lane = lax.broadcasted_iota(jnp.int32, (2 * sz.pair, LANES), 1)
        tile = jnp.where(lane == 0, high, jnp.where(lane == 1, middle, jnp.where(lane == 2, low, 0.0)))
        residual[:, early:] = tile.astype(BF)
        for message, flow in zip(messages, flows):
            message[:, : early + LANES] = residual[...]
            message[:, early + LANES :] = flow[...]


def backward_kernel(sz, chunk, step, *refs):
    scen = sz.scen
    parts, factors = refs[:scen], refs[scen]
    before = refs[scen + 1] if chunk else None
    last = chunk == CHUNKS - 1
    residual = refs[-1]
    outs = refs[scen + 1 + (chunk > 0) : -1]
    me, chip, core = where_am_i()
    if chunk == 0:
        balances = outs[-1]
        for slot in range(scen):

            @pl.when(chip == (me ^ slot))
            def _(slot=slot):
                tile = parts[slot][: sz.pair, sz.early : sz.early + LANES].astype(F32)
                found = jnp.sum(tile, axis=1, keepdims=True)
                balances[...] = jnp.broadcast_to(found, (sz.pair, LANES))

    widths = (sz.early,) if chunk == 0 else (sz.halves[0] - sz.early, sz.halves[1])
    for slot in range(scen):
        source = target = 0
        for width in widths:
            for side in range(2):
                residual[slot * sz.pair : (slot + 1) * sz.pair, target : target + width] = parts[slot][
                    side * sz.pair : (side + 1) * sz.pair, source : source + width
                ]
                target += width
            source += width

    def body(i, _):
        cols = pl.ds(pl.multiple_of(i * step, step), step)
        product, at = None, 0
        for low, high in sz.ranges[chunk]:
            term = jnp.dot(
                residual[:, at : at + high - low], factors[low:high, cols], preferred_element_type=F32
            )
            product = term if product is None else product + term
            at += high - low
        if chunk:
            product = before[:, cols] + product
        if not last:
            outs[0][:, cols] = product
            return 0
        kept, sent = outs[:2]
        even = [product[slot * sz.pair : slot * sz.pair + sz.rows] for slot in range(scen)]
        odd = [product[slot * sz.pair + sz.rows : (slot + 1) * sz.pair] for slot in range(scen)]
        even, odd = jnp.concatenate(even, 0), jnp.concatenate(odd, 0)
        kept[:, cols] = jnp.where(core == 0, even, odd)
        sent[:, cols] = jnp.where(core == 0, odd, even).astype(BF)
        return 0

    lax.fori_loop(0, sz.buses // step, body, 0)


def chip_kernel(sz, *refs):
    kept, received = refs[:2]
    outs, packed = refs[2:-1], refs[-1]
    scen, chip, core = where_am_i()
    total = kept[...] + received[...].astype(F32)
    for slot in range(sz.scen):
        for fold in range(sz.fold):
            packed[slot, fold * sz.rows : (fold + 1) * sz.rows, :] = total[
                slot * sz.rows : (slot + 1) * sz.rows, fold * sz.part : (fold + 1) * sz.part
            ]
    for away in range(sz.chips):
        found = packed[scen ^ chip ^ away]
        outs[away][...] = found.astype(outs[away].dtype)


def update_kernel(sz, last, *refs):
    parts = refs[: sz.chips]
    balances, lam, shed, loads, gens, select, costs, dual, previous, cap, commit = refs[sz.chips : sz.chips + 11]
    rest = refs[sz.chips + 11 :]
    core = where_am_i()[2]
    balance = jnp.where(core == 0, balances[: sz.rows, :1], balances[sz.rows :, :1])
    lam_now = lam[:, :1]
    shift = balance + lam_now
    shift = jnp.concatenate([shift] * sz.fold, 0)
    total = parts[0][...]
    for part in parts[1:]:
        total = total + part[...].astype(F32)
    grad = total + shift
    capacity = cap[...] * commit[...].astype(F32)
    if last:
        weights, gens_out, shed_out, lam_out, weighted_out, dual_out = rest
    else:
        gens_out, shed_out, lam_out, inject = rest
    lam_out[...] = jnp.broadcast_to(lam_now + balance, lam_out.shape)
    for block, rows, cols in blocks_of(sz):
        lanes = slice(block * LANES, (block + 1) * LANES)
        buses = slice(block * sz.width, (block + 1) * sz.width)
        load = loads[:, buses]
        shed_next = jnp.minimum(jnp.maximum(shed[:, buses] - 0.4 * (1.5 + grad[rows, cols]), 0.0), load)
        shed_out[:, buses] = shed_next
        picked = jnp.dot(stacked(grad[rows, cols]), select[block], preferred_element_type=F32)
        picked = unstacked(picked, sz.rows)
        now = gens[:, lanes]
        gen_grad = costs[:1, lanes] + costs[1:, lanes] * now + dual[:, lanes] + (now - previous[:, lanes]) + picked
        now = jnp.minimum(jnp.maximum(now - 0.4 * gen_grad, 0.0), capacity[:, lanes])
        gens_out[:, lanes] = now
        if last:
            dual_out[:, lanes] = dual[:, lanes] + now
            weighted_out[:1, lanes] = jnp.sum(weights[:, :1] * now, axis=0, keepdims=True)
            all_weights = jnp.sum(weights[:, :1], axis=0, keepdims=True)
            weighted_out[1:, lanes] = jnp.broadcast_to(all_weights, (7, LANES))
        else:
            inject[rows, cols] = (place(sz, now, select, block) + shed_next - load).astype(BF)


def add_kernel(first, second, out):
    out[...] = first[...] + second[...]


def finish_kernel(sz, *refs):
    parts = refs[: sz.chips]
    dual, consensus, dual_out = refs[sz.chips :]
    total = parts[0][...]
    for part in parts[1:]:
        total = total + part[...]
    mean = total[:1] / total[1:2]
    consensus[...] = mean
    dual_out[...] = dual[...] - mean


def to_scen(n, away, value):
    return lax.ppermute(value, "scen", [(i, i ^ away) for i in range(n)])


def to_chip(n, away, value):
    return lax.ppermute(value, "line", [(i, i ^ (2 * away)) for i in range(n)])


def spread(move, n, values):
    found = {away: move(n, away, values[away - 1]) for away in range(1, len(values) + 1)}
    return [found[away] for away in range(1, len(values) + 1)]


def to_core(n, value):
    return lax.ppermute(value, "line", [(i, i ^ 1) for i in range(n)])


def local(
    mesh,
    shift_factors,
    gen_bus,
    commit,
    cost_coef,
    gen_cap,
    bus_loads,
    load_shed,
    dispatch,
    ph_dual,
    consensus_prev,
    scen_weight,
    flow_copy,
    flow_dual,
    balance_dual,
    flow_limit,
):
    lines, buses = shift_factors.shape
    rows, gens = dispatch.shape
    sz = Sizes(mesh, lines, buses, gens, rows)
    n_scen, n_line, chips = sz.scen, sz.line, sz.chips
    row = lambda v: v.reshape(1, -1)
    column = lambda v: jnp.broadcast_to(v[:, None], (rows, LANES))
    capacity, on, previous, limits = row(gen_cap), row(commit), row(consensus_prev), row(flow_limit)
    lam, weights = column(balance_dual), column(scen_weight)
    packed = (sz.fold * rows, sz.part)
    step_b = next(s for s in (1024, 640, 512, 256, 128) if buses % s == 0)
    macs = [sz.total * 2 * half * buses for half in sz.halves]

    generation, copies, duals = dispatch, flow_copy, flow_dual
    first = (dispatch, load_shed - bus_loads, row(gen_bus))
    made = ((packed, BF), ((gens // LANES, sz.width, LANES), BF))
    shed = load_shed
    inject, select = call(
        functools.partial(start_kernel, sz),
        first,
        made,
        flops=1000 * lines * buses,
        limit=GRANT - nbytes(first + tuple(jax.ShapeDtypeStruct(*each) for each in made)) - (1 << 16),
    )
    for iteration in range(ITERS):
        own = [inject] + spread(to_chip, n_line, [inject] * (chips - 1))
        other = [to_core(n_line, value) for value in own]
        final = iteration == ITERS - 1
        tall = 2 * sz.pair
        widths = (sz.halves[0] + LANES, sz.halves[1])
        flows = []
        for chunk in range(CHUNKS):
            block = (tall, widths[chunk])
            flows.append(
                call(
                    functools.partial(forward_kernel, sz, chunk),
                    (*own, *other, shift_factors),
                    [(block, F32)] + [(block, BF)] * (n_scen - 1),
                    [((sz.total, buses), BF), ((chips, *block), F32)],
                    flops=2 * macs[chunk],
                    limit=GRANT - (nbytes(own + other) if iteration == 0 else 0),
                )
            )
            if chunk == 0:
                parts = [flows[0][0]] + spread(to_scen, n_scen, flows[0][1:])
        state = lambda width: [((sz.pair, width), F32)] * 2
        old = (flow_copy, flow_dual) if iteration == 0 else None
        first_res, rest, first_copy, first_dual, *messages = call(
            functools.partial(residual_kernel, sz, 0),
            (*parts, *(old or (copies[0], duals[0])), limits, *flows[1][1:]),
            [
                ((tall, sz.early + LANES), BF),
                ((tall, sz.halves[0] - sz.early), BF),
                *state(2 * sz.halves[0]),
                *[((tall, sz.early + LANES + sz.halves[1]), BF)] * (n_scen - 1),
            ],
            keep=shift_factors,
        )
        got = spread(to_scen, n_scen, messages)
        second_res, second_copy, second_dual = call(
            functools.partial(residual_kernel, sz, 1),
            (
                flows[1][0],
                *got,
                *(old or (copies[1], duals[1])),
                limits,
                rest,
            ),
            [((tall, lines // 2 - sz.early), BF), *state(2 * sz.halves[1])],
            keep=shift_factors,
        )
        residuals = [
            [first_res, *got],
            [second_res] + spread(to_scen, n_scen, [second_res] * (n_scen - 1)),
        ]
        new_copies, new_duals = [first_copy, second_copy], [first_dual, second_dual]
        copies, duals = new_copies, new_duals
        before, balances = (), None
        for chunk in range(CHUNKS):
            last = chunk == CHUNKS - 1
            half = (sz.total // 2, buses)
            outs = [(half, F32), (half, BF)] if last else [((sz.total, buses), F32)]
            if chunk == 0:
                outs.append(((sz.pair, LANES), F32))
            found = call(
                functools.partial(backward_kernel, sz, chunk, step_b),
                (*residuals[chunk], shift_factors, *before),
                outs,
                [((sz.total, sum(high - low for low, high in sz.ranges[chunk])), BF)],
                flops=sum(macs),
            )
            if chunk == 0:
                balances = found[-1]
            before = found[:1]
        kept, sent = found[:2]
        sums = call(
            functools.partial(chip_kernel, sz),
            (kept, to_core(n_line, sent)),
            [(packed, F32)] + [(packed, BF)] * (chips - 1),
            [((chips, *packed), F32)],
            keep=None if final else shift_factors,
        )
        parts = [sums[0]] + spread(to_chip, n_line, sums[1:])
        args = (*parts, balances, lam, shed, bus_loads, generation, select, cost_coef, ph_dual, previous, capacity, on)
        if not final:
            generation, shed, lam, inject = call(
                functools.partial(update_kernel, sz, False),
                args,
                [((rows, gens), F32), ((rows, buses), F32), ((rows, LANES), F32), (packed, BF)],
                keep=shift_factors,
                limit=GRANT - nbytes((dispatch, select)),
            )
        else:
            generation, shed, lam, weighted, dual_sum = call(
                functools.partial(update_kernel, sz, True),
                (*args, weights),
                [((rows, gens), F32), ((rows, buses), F32), ((rows, LANES), F32), ((8, gens), F32), ((rows, gens), F32)],
            )
    (weighted,) = call(add_kernel, (weighted, to_core(n_line, weighted)), [((8, gens), F32)])
    parts = [weighted] + spread(to_chip, n_line, [weighted] * (chips - 1))
    consensus, dual_out = call(
        functools.partial(finish_kernel, sz),
        (*parts, dual_sum),
        [((1, gens), F32), ((rows, gens), F32)],
    )
    return generation, shed, jnp.concatenate(copies, 1), jnp.concatenate(duals, 1), lam[:, 0], consensus.reshape(-1), dual_out


def solution(mesh):
    return jax.shard_map(
        functools.partial(local, mesh),
        mesh=mesh,
        in_specs=(
            P("line", "scen"),
            P("scen"),
            P("scen"),
            P(None, "scen"),
            P("scen"),
            P("line", "scen"),
            P("line", "scen"),
            P("line", "scen"),
            P("line", "scen"),
            P("scen"),
            P("line"),
            P("scen", "line"),
            P("scen", "line"),
            P("line"),
            P("line"),
        ),
        out_specs=(
            P("line", "scen"),
            P("line", "scen"),
            P("scen", "line"),
            P("scen", "line"),
            P("line"),
            P("scen"),
            P("line", "scen"),
        ),
        check_vma=False,
    )
```

```python
import functools
import math

import jax
import jax.numpy as jnp
from jax import lax
from jax.experimental import pallas as pl
from jax.experimental.pallas import tpu as pltpu
from jax.sharding import PartitionSpec as P

BUSES = 20480
ITERS = 2
CHUNKS = 2
FIRST_SHARE = 0.5625
EARLY_SHARE = 0.4375
LANES = 128
GRANT = 11 << 20
BF = jnp.bfloat16
F32 = jnp.float32
WHOLE = pl.BlockSpec(memory_space=pltpu.VMEM)


def call(kernel, args, outs, scratch=(), flops=0, keep=None, limit=GRANT):
    size = sum(a.size * a.dtype.itemsize for a in args)
    if keep is not None:
        inner, args = kernel, (keep, *args)
        kernel = lambda kept, *refs: inner(*refs)
    return pl.pallas_call(
        kernel,
        in_specs=[WHOLE] * len(args),
        out_specs=[WHOLE] * len(outs),
        out_shape=[jax.ShapeDtypeStruct(shape, kind) for shape, kind in outs],
        scratch_shapes=[pltpu.VMEM(shape, kind) for shape, kind in scratch],
        compiler_params=pltpu.CompilerParams(vmem_limit_bytes=limit),
        cost_estimate=pl.CostEstimate(flops=flops, bytes_accessed=size, transcendentals=0),
    )(*args)


def nbytes(arrays):
    size = lambda a: math.prod(a.shape[:-2]) * -(-a.shape[-2] // 8) * 8 * a.shape[-1] * a.dtype.itemsize
    return sum(size(a) for a in arrays)


def pieces(value):
    high = value.astype(BF)
    rest = value - high.astype(F32)
    middle = rest.astype(BF)
    low = (rest - middle.astype(F32)).astype(BF)
    return high, middle, low


def stacked(value):
    rows, columns = value.shape
    below = [jnp.zeros((8 - rows, columns), F32)] if rows < 8 else []
    parts = []
    for piece in pieces(value):
        parts += [piece.astype(F32)] + below
    return jnp.concatenate(parts, 0).astype(BF)


def unstacked(product, rows):
    return (product[16 : 16 + rows] + product[8 : 8 + rows]) + product[:rows]


def dot_t(a, b):
    return lax.dot_general(a, b, (((1,), (1,)), ((), ())), preferred_element_type=F32)


class Sizes:
    def __init__(self, mesh, lines, buses, gens, rows):
        self.scen = mesh.shape["scen"]
        self.line = mesh.shape["line"]
        self.chips = self.line // 2
        assert self.chips == self.scen
        self.lines, self.buses, self.gens, self.rows = lines, buses, gens, rows
        self.pair = 2 * rows
        self.total = rows * self.line
        self.stretch = buses // gens
        self.width = self.stretch * LANES
        self.fold = next(f for f in (4, 2, 1) if buses % (f * self.width) == 0)
        self.part = buses // self.fold
        tiles = lambda share, least, most: min(max(round(share * lines / 2 / LANES), least), most) * LANES
        first = tiles(FIRST_SHARE, 2, lines // 2 // LANES - 1)
        self.halves = (first, lines // 2 - first)
        self.early = tiles(EARLY_SHARE, 1, first // LANES - 1)
        self.starts = (0, 2 * first)
        self.ranges = (((0, self.early), (first, first + self.early)), ((self.early, first), (first + self.early, lines)))


def where_am_i():
    line = lax.axis_index("line")
    return lax.axis_index("scen"), lax.div(line, 2), lax.rem(line, 2)


def place(sz, gens, select):
    pile = stacked(gens)
    blocks = [dot_t(pile[:, block * LANES : (block + 1) * LANES], select[block]) for block in range(sz.gens // LANES)]
    return [unstacked(product, sz.rows) for product in blocks]


def blocks_of(sz):
    per = sz.part // sz.width
    for block in range(sz.gens // LANES):
        fold, inner = divmod(block, per)
        yield block, slice(fold * sz.rows, (fold + 1) * sz.rows), slice(inner * sz.width, (inner + 1) * sz.width)


def start_kernel(sz, dispatch, net, gen_bus, inject, select):
    first = lax.axis_index("scen") * sz.buses
    bus = lax.broadcasted_iota(jnp.int32, (sz.width, LANES), 0)
    for block, rows, cols in blocks_of(sz):
        lanes = slice(block * LANES, (block + 1) * LANES)
        local = gen_bus[:, lanes] - (first + block * sz.width)
        select[block] = (bus == local).astype(F32).astype(BF)
    placed = place(sz, dispatch[...], select)
    for block, rows, cols in blocks_of(sz):
        inject[rows, cols] = (placed[block] + net[:, block * sz.width : (block + 1) * sz.width]).astype(BF)


def forward_kernel(sz, chunk, *refs):
    chips = sz.chips
    own, other = refs[:chips], refs[chips : 2 * chips]
    factors = refs[2 * chips]
    outs = refs[2 * chips + 1 : 3 * chips + 1]
    inject, flows = refs[3 * chips + 1 :]
    scen, chip, core = where_am_i()
    half = sz.halves[chunk]

    def gather(first, second):
        for slot in range(chips):
            for fold in range(sz.fold):
                rows = slice(fold * sz.rows, (fold + 1) * sz.rows)
                cols = slice(fold * sz.part, (fold + 1) * sz.part)
                base = slot * sz.pair
                inject[base : base + sz.rows, cols] = first[slot][rows, :]
                inject[base + sz.rows : base + sz.pair, cols] = second[slot][rows, :]

    @pl.when(core == 0)
    def _():
        gather(own, other)

    @pl.when(core == 1)
    def _():
        gather(other, own)

    if chunk == 0:
        total = jnp.sum(inject[...].astype(F32), axis=1, keepdims=True)
        high, middle, low = (piece.astype(F32) for piece in pieces(total))
        lane = lax.broadcasted_iota(jnp.int32, (sz.total, LANES), 1)
        tile = jnp.where(lane == 0, high, jnp.where(lane == 1, middle, jnp.where(lane == 2, low, 0.0)))
        for slot in range(chips):
            flows[slot, :, half:] = jnp.zeros((2 * sz.pair, LANES), F32)
            flows[slot, : sz.pair, half:] = tile[slot * sz.pair : (slot + 1) * sz.pair]
    for side in range(2):
        start = sz.starts[chunk] + side * half
        product = dot_t(factors[start : start + half, :], inject[...]).T
        for slot in range(chips):
            flows[slot, side * sz.pair : (side + 1) * sz.pair, :half] = product[slot * sz.pair : (slot + 1) * sz.pair]
    for away in range(chips):
        found = flows[chip ^ scen ^ away]
        outs[away][...] = found.astype(outs[away].dtype)


def residual_kernel(sz, chunk, *refs):
    scen = sz.scen
    half, early, start = sz.halves[chunk], sz.early, sz.starts[chunk]
    parts = refs[:scen]
    copies, duals, limits = refs[scen : scen + 3]
    if chunk == 0:
        flows = refs[scen + 3 : 2 * scen + 2]
        residual, rest, copy_out, dual_out = refs[2 * scen + 2 : 2 * scen + 6]
        messages = refs[2 * scen + 6 :]
        skip = 0
    else:
        rest, residual, copy_out, dual_out = refs[scen + 3 :]
        before = rest.shape[1]
        residual[:, :before] = rest[...]
        skip = early + LANES
    total = parts[0][...]
    for part in parts[1:]:
        total = total + part[:, skip:].astype(F32)
    for side in range(2):
        rows = slice(side * sz.pair, (side + 1) * sz.pair)
        base = start if copies.shape[1] == sz.lines else 0
        cols = slice(base + side * half, base + (side + 1) * half)
        to = slice(side * half, (side + 1) * half)
        now, copy, dual = total[rows, :half], copies[:, cols], duals[:, cols]
        limit = limits[:, start + side * half : start + (side + 1) * half]
        found = (now - copy + dual).astype(BF)
        if chunk == 0:
            residual[rows, :early] = found[:, :early]
            rest[rows, :] = found[:, early:]
        else:
            residual[rows, before:] = found
        copy_next = jnp.minimum(jnp.maximum(now + dual, -limit), limit)
        copy_out[:, to] = copy_next
        dual_out[:, to] = dual + now - copy_next
    if chunk == 0:
        balance = jnp.sum(total[:, half:], axis=1, keepdims=True) / BUSES
        high, middle, low = (piece.astype(F32) for piece in pieces(balance))
        lane = lax.broadcasted_iota(jnp.int32, (2 * sz.pair, LANES), 1)
        tile = jnp.where(lane == 0, high, jnp.where(lane == 1, middle, jnp.where(lane == 2, low, 0.0)))
        residual[:, early:] = tile.astype(BF)
        for message, flow in zip(messages, flows):
            message[:, : early + LANES] = residual[...]
            message[:, early + LANES :] = flow[...]


def backward_kernel(sz, chunk, step, *refs):
    scen = sz.scen
    parts, factors = refs[:scen], refs[scen]
    before = refs[scen + 1] if chunk else None
    last = chunk == CHUNKS - 1
    residual = refs[-1]
    outs = refs[scen + 1 + (chunk > 0) : -1]
    me, chip, core = where_am_i()
    if chunk == 0:
        balances = outs[-1]
        for slot in range(scen):

            @pl.when(chip == (me ^ slot))
            def _(slot=slot):
                tile = parts[slot][: sz.pair, sz.early : sz.early + LANES].astype(F32)
                found = jnp.sum(tile, axis=1, keepdims=True)
                balances[...] = jnp.broadcast_to(found, (sz.pair, LANES))

    widths = (sz.early,) if chunk == 0 else (sz.halves[0] - sz.early, sz.halves[1])
    for slot in range(scen):
        source = target = 0
        for width in widths:
            for side in range(2):
                residual[slot * sz.pair : (slot + 1) * sz.pair, target : target + width] = parts[slot][
                    side * sz.pair : (side + 1) * sz.pair, source : source + width
                ]
                target += width
            source += width

    def body(i, _):
        cols = pl.ds(pl.multiple_of(i * step, step), step)
        product, at = None, 0
        for low, high in sz.ranges[chunk]:
            term = jnp.dot(
                residual[:, at : at + high - low], factors[low:high, cols], preferred_element_type=F32
            )
            product = term if product is None else product + term
            at += high - low
        if chunk:
            product = before[:, cols] + product
        if not last:
            outs[0][:, cols] = product
            return 0
        kept, sent = outs[:2]
        even = [product[slot * sz.pair : slot * sz.pair + sz.rows] for slot in range(scen)]
        odd = [product[slot * sz.pair + sz.rows : (slot + 1) * sz.pair] for slot in range(scen)]
        even, odd = jnp.concatenate(even, 0), jnp.concatenate(odd, 0)
        kept[:, cols] = jnp.where(core == 0, even, odd)
        sent[:, cols] = jnp.where(core == 0, odd, even).astype(BF)
        return 0

    lax.fori_loop(0, sz.buses // step, body, 0)


def chip_kernel(sz, *refs):
    kept, received = refs[:2]
    outs, packed = refs[2:-1], refs[-1]
    scen, chip, core = where_am_i()
    total = kept[...] + received[...].astype(F32)
    for slot in range(sz.scen):
        for fold in range(sz.fold):
            packed[slot, fold * sz.rows : (fold + 1) * sz.rows, :] = total[
                slot * sz.rows : (slot + 1) * sz.rows, fold * sz.part : (fold + 1) * sz.part
            ]
    for away in range(sz.chips):
        found = packed[scen ^ chip ^ away]
        outs[away][...] = found.astype(outs[away].dtype)


def update_kernel(sz, last, *refs):
    parts = refs[: sz.chips]
    balances, lam, shed, loads, gens, select, costs, dual, previous, cap, commit = refs[sz.chips : sz.chips + 11]
    rest = refs[sz.chips + 11 :]
    core = where_am_i()[2]
    balance = jnp.where(core == 0, balances[: sz.rows, :1], balances[sz.rows :, :1])
    lam_now = lam[:, :1]
    shift = balance + lam_now
    shift = jnp.concatenate([shift] * sz.fold, 0)
    total = parts[0][...]
    for part in parts[1:]:
        total = total + part[...].astype(F32)
    grad = total + shift
    capacity = cap[...] * commit[...].astype(F32)
    if last:
        weights, gens_out, shed_out, lam_out, weighted_out, dual_out = rest
    else:
        gens_out, shed_out, lam_out, inject = rest
    lam_out[...] = jnp.broadcast_to(lam_now + balance, lam_out.shape)
    piles = [stacked(grad[fold * sz.rows : (fold + 1) * sz.rows]) for fold in range(sz.fold)]
    picked = [
        unstacked(jnp.dot(piles[rows.start // sz.rows][:, cols], select[block], preferred_element_type=F32), sz.rows)
        for block, rows, cols in blocks_of(sz)
    ]
    picked = jnp.concatenate(picked, 1)
    now = gens[...]
    gen_grad = costs[:1] + costs[1:] * now + dual[...] + (now - previous[...]) + picked
    now = jnp.minimum(jnp.maximum(now - 0.4 * gen_grad, 0.0), capacity)
    gens_out[...] = now
    if last:
        dual_out[...] = dual[...] + now
        weighted_out[:1] = jnp.sum(weights[:, :1] * now, axis=0, keepdims=True)
        all_weights = jnp.sum(weights[:, :1], axis=0, keepdims=True)
        weighted_out[1:] = jnp.broadcast_to(all_weights, (7, sz.gens))
    else:
        placed = place(sz, now, select)
    for block, rows, cols in blocks_of(sz):
        buses = slice(block * sz.width, (block + 1) * sz.width)
        load = loads[:, buses]
        shed_next = jnp.minimum(jnp.maximum(shed[:, buses] - 0.4 * (1.5 + grad[rows, cols]), 0.0), load)
        shed_out[:, buses] = shed_next
        if not last:
            inject[rows, cols] = (placed[block] + shed_next - load).astype(BF)


def add_kernel(first, second, out):
    out[...] = first[...] + second[...]


def finish_kernel(sz, *refs):
    parts = refs[: sz.chips]
    dual, consensus, dual_out = refs[sz.chips :]
    total = parts[0][...]
    for part in parts[1:]:
        total = total + part[...]
    mean = total[:1] / total[1:2]
    consensus[...] = mean
    dual_out[...] = dual[...] - mean


def to_scen(n, away, value):
    return lax.ppermute(value, "scen", [(i, i ^ away) for i in range(n)])


def to_chip(n, away, value):
    return lax.ppermute(value, "line", [(i, i ^ (2 * away)) for i in range(n)])


def spread(move, n, values):
    found = {away: move(n, away, values[away - 1]) for away in range(1, len(values) + 1)}
    return [found[away] for away in range(1, len(values) + 1)]


def to_core(n, value):
    return lax.ppermute(value, "line", [(i, i ^ 1) for i in range(n)])


def local(
    mesh,
    shift_factors,
    gen_bus,
    commit,
    cost_coef,
    gen_cap,
    bus_loads,
    load_shed,
    dispatch,
    ph_dual,
    consensus_prev,
    scen_weight,
    flow_copy,
    flow_dual,
    balance_dual,
    flow_limit,
):
    lines, buses = shift_factors.shape
    rows, gens = dispatch.shape
    sz = Sizes(mesh, lines, buses, gens, rows)
    n_scen, n_line, chips = sz.scen, sz.line, sz.chips
    row = lambda v: v.reshape(1, -1)
    column = lambda v: jnp.broadcast_to(v[:, None], (rows, LANES))
    capacity, on, previous, limits = row(gen_cap), row(commit), row(consensus_prev), row(flow_limit)
    lam, weights = column(balance_dual), column(scen_weight)
    packed = (sz.fold * rows, sz.part)
    step_b = next(s for s in (1024, 640, 512, 256, 128) if buses % s == 0)
    macs = [sz.total * 2 * half * buses for half in sz.halves]

    generation, copies, duals = dispatch, flow_copy, flow_dual
    first = (dispatch, load_shed - bus_loads, row(gen_bus))
    made = ((packed, BF), ((gens // LANES, sz.width, LANES), BF))
    shed = load_shed
    inject, select = call(
        functools.partial(start_kernel, sz),
        first,
        made,
        flops=1000 * lines * buses,
        limit=GRANT - nbytes(first + tuple(jax.ShapeDtypeStruct(*each) for each in made)) - (1 << 16),
    )
    for iteration in range(ITERS):
        own = [inject] + spread(to_chip, n_line, [inject] * (chips - 1))
        other = [to_core(n_line, value) for value in own]
        final = iteration == ITERS - 1
        tall = 2 * sz.pair
        widths = (sz.halves[0] + LANES, sz.halves[1])
        flows = []
        for chunk in range(CHUNKS):
            block = (tall, widths[chunk])
            flows.append(
                call(
                    functools.partial(forward_kernel, sz, chunk),
                    (*own, *other, shift_factors),
                    [(block, F32)] + [(block, BF)] * (n_scen - 1),
                    [((sz.total, buses), BF), ((chips, *block), F32)],
                    flops=2 * macs[chunk],
                    limit=GRANT - (nbytes(own + other) if iteration == 0 else 0),
                )
            )
            if chunk == 0:
                parts = [flows[0][0]] + spread(to_scen, n_scen, flows[0][1:])
        state = lambda width: [((sz.pair, width), F32)] * 2
        old = (flow_copy, flow_dual) if iteration == 0 else None
        first_res, rest, first_copy, first_dual, *messages = call(
            functools.partial(residual_kernel, sz, 0),
            (*parts, *(old or (copies[0], duals[0])), limits, *flows[1][1:]),
            [
                ((tall, sz.early + LANES), BF),
                ((tall, sz.halves[0] - sz.early), BF),
                *state(2 * sz.halves[0]),
                *[((tall, sz.early + LANES + sz.halves[1]), BF)] * (n_scen - 1),
            ],
            keep=shift_factors,
        )
        got = spread(to_scen, n_scen, messages)
        second_res, second_copy, second_dual = call(
            functools.partial(residual_kernel, sz, 1),
            (
                flows[1][0],
                *got,
                *(old or (copies[1], duals[1])),
                limits,
                rest,
            ),
            [((tall, lines // 2 - sz.early), BF), *state(2 * sz.halves[1])],
            keep=shift_factors,
        )
        residuals = [
            [first_res, *got],
            [second_res] + spread(to_scen, n_scen, [second_res] * (n_scen - 1)),
        ]
        new_copies, new_duals = [first_copy, second_copy], [first_dual, second_dual]
        copies, duals = new_copies, new_duals
        before, balances = (), None
        for chunk in range(CHUNKS):
            last = chunk == CHUNKS - 1
            half = (sz.total // 2, buses)
            outs = [(half, F32), (half, BF)] if last else [((sz.total, buses), F32)]
            if chunk == 0:
                outs.append(((sz.pair, LANES), F32))
            found = call(
                functools.partial(backward_kernel, sz, chunk, step_b),
                (*residuals[chunk], shift_factors, *before),
                outs,
                [((sz.total, sum(high - low for low, high in sz.ranges[chunk])), BF)],
                flops=sum(macs),
            )
            if chunk == 0:
                balances = found[-1]
            before = found[:1]
        kept, sent = found[:2]
        sums = call(
            functools.partial(chip_kernel, sz),
            (kept, to_core(n_line, sent)),
            [(packed, F32)] + [(packed, BF)] * (chips - 1),
            [((chips, *packed), F32)],
            keep=None if final else shift_factors,
        )
        parts = [sums[0]] + spread(to_chip, n_line, sums[1:])
        args = (*parts, balances, lam, shed, bus_loads, generation, select, cost_coef, ph_dual, previous, capacity, on)
        if not final:
            generation, shed, lam, inject = call(
                functools.partial(update_kernel, sz, False),
                args,
                [((rows, gens), F32), ((rows, buses), F32), ((rows, LANES), F32), (packed, BF)],
                keep=shift_factors,
                limit=GRANT - nbytes((dispatch, select)),
            )
        else:
            generation, shed, lam, weighted, dual_sum = call(
                functools.partial(update_kernel, sz, True),
                (*args, weights),
                [((rows, gens), F32), ((rows, buses), F32), ((rows, LANES), F32), ((8, gens), F32), ((rows, gens), F32)],
            )
    (weighted,) = call(add_kernel, (weighted, to_core(n_line, weighted)), [((8, gens), F32)])
    parts = [weighted] + spread(to_chip, n_line, [weighted] * (chips - 1))
    consensus, dual_out = call(
        functools.partial(finish_kernel, sz),
        (*parts, dual_sum),
        [((1, gens), F32), ((rows, gens), F32)],
    )
    return generation, shed, jnp.concatenate(copies, 1), jnp.concatenate(duals, 1), lam[:, 0], consensus.reshape(-1), dual_out


def solution(mesh):
    return jax.shard_map(
        functools.partial(local, mesh),
        mesh=mesh,
        in_specs=(
            P("line", "scen"),
            P("scen"),
            P("scen"),
            P(None, "scen"),
            P("scen"),
            P("line", "scen"),
            P("line", "scen"),
            P("line", "scen"),
            P("line", "scen"),
            P("scen"),
            P("line"),
            P("scen", "line"),
            P("scen", "line"),
            P("line"),
            P("line"),
        ),
        out_specs=(
            P("line", "scen"),
            P("line", "scen"),
            P("scen", "line"),
            P("scen", "line"),
            P("line"),
            P("scen"),
            P("line", "scen"),
        ),
        check_vma=False,
    )
```

```python
import functools
import math

import jax
import jax.numpy as jnp
from jax import lax
from jax.experimental import pallas as pl
from jax.experimental.pallas import tpu as pltpu
from jax.sharding import PartitionSpec as P

BUSES = 20480
ITERS = 2
CHUNKS = 2
FIRST_SHARE = 0.5
EARLY_SHARE = 0.4375
LANES = 128
GRANT = 11 << 20
BF = jnp.bfloat16
F32 = jnp.float32
WHOLE = pl.BlockSpec(memory_space=pltpu.VMEM)


def call(kernel, args, outs, scratch=(), flops=0, keep=None, limit=GRANT):
    size = sum(a.size * a.dtype.itemsize for a in args)
    if keep is not None:
        inner, args = kernel, (keep, *args)
        kernel = lambda kept, *refs: inner(*refs)
    return pl.pallas_call(
        kernel,
        in_specs=[WHOLE] * len(args),
        out_specs=[WHOLE] * len(outs),
        out_shape=[jax.ShapeDtypeStruct(shape, kind) for shape, kind in outs],
        scratch_shapes=[pltpu.VMEM(shape, kind) for shape, kind in scratch],
        compiler_params=pltpu.CompilerParams(vmem_limit_bytes=limit),
        cost_estimate=pl.CostEstimate(flops=flops, bytes_accessed=size, transcendentals=0),
    )(*args)


def nbytes(arrays):
    size = lambda a: math.prod(a.shape[:-2]) * -(-a.shape[-2] // 8) * 8 * a.shape[-1] * a.dtype.itemsize
    return sum(size(a) for a in arrays)


def pieces(value):
    high = value.astype(BF)
    rest = value - high.astype(F32)
    middle = rest.astype(BF)
    low = (rest - middle.astype(F32)).astype(BF)
    return high, middle, low


def stacked(value):
    rows, columns = value.shape
    below = [jnp.zeros((8 - rows, columns), F32)] if rows < 8 else []
    parts = []
    for piece in pieces(value):
        parts += [piece.astype(F32)] + below
    return jnp.concatenate(parts, 0).astype(BF)


def unstacked(product, rows):
    return (product[16 : 16 + rows] + product[8 : 8 + rows]) + product[:rows]


def dot_t(a, b):
    return lax.dot_general(a, b, (((1,), (1,)), ((), ())), preferred_element_type=F32)


class Sizes:
    def __init__(self, mesh, lines, buses, gens, rows):
        self.scen = mesh.shape["scen"]
        self.line = mesh.shape["line"]
        self.chips = self.line // 2
        assert self.chips == self.scen
        self.lines, self.buses, self.gens, self.rows = lines, buses, gens, rows
        self.pair = 2 * rows
        self.total = rows * self.line
        self.stretch = buses // gens
        self.width = self.stretch * LANES
        self.fold = next(f for f in (4, 2, 1) if buses % (f * self.width) == 0)
        self.part = buses // self.fold
        tiles = lambda share, least, most: min(max(round(share * lines / 2 / LANES), least), most) * LANES
        first = tiles(FIRST_SHARE, 2, lines // 2 // LANES - 1)
        self.halves = (first, lines // 2 - first)
        self.early = tiles(EARLY_SHARE, 1, first // LANES - 1)
        self.starts = (0, 2 * first)
        self.ranges = (((0, self.early), (first, first + self.early)), ((self.early, first), (first + self.early, lines)))


def where_am_i():
    line = lax.axis_index("line")
    return lax.axis_index("scen"), lax.div(line, 2), lax.rem(line, 2)


def place(sz, gens, select):
    pile = stacked(gens)
    blocks = [dot_t(pile[:, block * LANES : (block + 1) * LANES], select[block]) for block in range(sz.gens // LANES)]
    return [unstacked(product, sz.rows) for product in blocks]


def blocks_of(sz):
    per = sz.part // sz.width
    for block in range(sz.gens // LANES):
        fold, inner = divmod(block, per)
        yield block, slice(fold * sz.rows, (fold + 1) * sz.rows), slice(inner * sz.width, (inner + 1) * sz.width)


def start_kernel(sz, dispatch, net, gen_bus, inject, select):
    first = lax.axis_index("scen") * sz.buses
    bus = lax.broadcasted_iota(jnp.int32, (sz.width, LANES), 0)
    for block, rows, cols in blocks_of(sz):
        lanes = slice(block * LANES, (block + 1) * LANES)
        local = gen_bus[:, lanes] - (first + block * sz.width)
        select[block] = (bus == local).astype(F32).astype(BF)
    placed = place(sz, dispatch[...], select)
    for block, rows, cols in blocks_of(sz):
        inject[rows, cols] = (placed[block] + net[:, block * sz.width : (block + 1) * sz.width]).astype(BF)


def forward_kernel(sz, chunk, *refs):
    chips = sz.chips
    own, other = refs[:chips], refs[chips : 2 * chips]
    factors = refs[2 * chips]
    outs = refs[2 * chips + 1 : 3 * chips + 1]
    inject, flows = refs[3 * chips + 1 :]
    scen, chip, core = where_am_i()
    half = sz.halves[chunk]

    def gather(first, second):
        for slot in range(chips):
            for fold in range(sz.fold):
                rows = slice(fold * sz.rows, (fold + 1) * sz.rows)
                cols = slice(fold * sz.part, (fold + 1) * sz.part)
                base = slot * sz.pair
                inject[base : base + sz.rows, cols] = first[slot][rows, :]
                inject[base + sz.rows : base + sz.pair, cols] = second[slot][rows, :]

    @pl.when(core == 0)
    def _():
        gather(own, other)

    @pl.when(core == 1)
    def _():
        gather(other, own)

    if chunk == 0:
        total = jnp.sum(inject[...].astype(F32), axis=1, keepdims=True)
        high, middle, low = (piece.astype(F32) for piece in pieces(total))
        lane = lax.broadcasted_iota(jnp.int32, (sz.total, LANES), 1)
        tile = jnp.where(lane == 0, high, jnp.where(lane == 1, middle, jnp.where(lane == 2, low, 0.0)))
        for slot in range(chips):
            flows[slot, :, half:] = jnp.zeros((2 * sz.pair, LANES), F32)
            flows[slot, : sz.pair, half:] = tile[slot * sz.pair : (slot + 1) * sz.pair]
    for side in range(2):
        start = sz.starts[chunk] + side * half
        product = dot_t(factors[start : start + half, :], inject[...]).T
        for slot in range(chips):
            flows[slot, side * sz.pair : (side + 1) * sz.pair, :half] = product[slot * sz.pair : (slot + 1) * sz.pair]
    for away in range(chips):
        found = flows[chip ^ scen ^ away]
        outs[away][...] = found.astype(outs[away].dtype)


def residual_kernel(sz, chunk, *refs):
    scen = sz.scen
    half, early, start = sz.halves[chunk], sz.early, sz.starts[chunk]
    parts = refs[:scen]
    copies, duals, limits = refs[scen : scen + 3]
    if chunk == 0:
        residual, rest, copy_out, dual_out = refs[scen + 4 :]
    else:
        rest, residual, copy_out, dual_out = refs[scen + 3 :]
        before = rest.shape[1]
        residual[:, :before] = rest[...]
    total = parts[0][...]
    for part in parts[1:]:
        total = total + part[...].astype(F32)
    for side in range(2):
        rows = slice(side * sz.pair, (side + 1) * sz.pair)
        base = start if copies.shape[1] == sz.lines else 0
        cols = slice(base + side * half, base + (side + 1) * half)
        to = slice(side * half, (side + 1) * half)
        now, copy, dual = total[rows, :half], copies[:, cols], duals[:, cols]
        limit = limits[:, start + side * half : start + (side + 1) * half]
        found = (now - copy + dual).astype(BF)
        if chunk == 0:
            residual[rows, :early] = found[:, :early]
            rest[rows, :] = found[:, early:]
        else:
            residual[rows, before:] = found
        copy_next = jnp.minimum(jnp.maximum(now + dual, -limit), limit)
        copy_out[:, to] = copy_next
        dual_out[:, to] = dual + now - copy_next
    if chunk == 0:
        balance = jnp.sum(total[:, half:], axis=1, keepdims=True) / BUSES
        high, middle, low = (piece.astype(F32) for piece in pieces(balance))
        lane = lax.broadcasted_iota(jnp.int32, (2 * sz.pair, LANES), 1)
        tile = jnp.where(lane == 0, high, jnp.where(lane == 1, middle, jnp.where(lane == 2, low, 0.0)))
        residual[:, early:] = tile.astype(BF)


def backward_kernel(sz, chunk, step, *refs):
    scen = sz.scen
    parts, factors = refs[:scen], refs[scen]
    before = refs[scen + 1] if chunk else None
    last = chunk == CHUNKS - 1
    residual = refs[-1]
    outs = refs[scen + 1 + (chunk > 0) : -1]
    me, chip, core = where_am_i()
    if chunk == 0:
        balances = outs[-1]
        for slot in range(scen):

            @pl.when(chip == (me ^ slot))
            def _(slot=slot):
                tile = parts[slot][: sz.pair, sz.early : sz.early + LANES].astype(F32)
                found = jnp.sum(tile, axis=1, keepdims=True)
                balances[...] = jnp.broadcast_to(found, (sz.pair, LANES))

    widths = (sz.early,) if chunk == 0 else (sz.halves[0] - sz.early, sz.halves[1])
    for slot in range(scen):
        source = target = 0
        for width in widths:
            for side in range(2):
                residual[slot * sz.pair : (slot + 1) * sz.pair, target : target + width] = parts[slot][
                    side * sz.pair : (side + 1) * sz.pair, source : source + width
                ]
                target += width
            source += width

    def body(i, _):
        cols = pl.ds(pl.multiple_of(i * step, step), step)
        product, at = None, 0
        for low, high in sz.ranges[chunk]:
            term = jnp.dot(
                residual[:, at : at + high - low], factors[low:high, cols], preferred_element_type=F32
            )
            product = term if product is None else product + term
            at += high - low
        if chunk:
            product = before[:, cols] + product
        if not last:
            outs[0][:, cols] = product
            return 0
        kept, sent = outs[:2]
        even = [product[slot * sz.pair : slot * sz.pair + sz.rows] for slot in range(scen)]
        odd = [product[slot * sz.pair + sz.rows : (slot + 1) * sz.pair] for slot in range(scen)]
        even, odd = jnp.concatenate(even, 0), jnp.concatenate(odd, 0)
        kept[:, cols] = jnp.where(core == 0, even, odd)
        sent[:, cols] = jnp.where(core == 0, odd, even).astype(BF)
        return 0

    lax.fori_loop(0, sz.buses // step, body, 0)


def chip_kernel(sz, *refs):
    kept, received = refs[:2]
    outs, packed = refs[2:-1], refs[-1]
    scen, chip, core = where_am_i()
    total = kept[...] + received[...].astype(F32)
    for slot in range(sz.scen):
        for fold in range(sz.fold):
            packed[slot, fold * sz.rows : (fold + 1) * sz.rows, :] = total[
                slot * sz.rows : (slot + 1) * sz.rows, fold * sz.part : (fold + 1) * sz.part
            ]
    for away in range(sz.chips):
        found = packed[scen ^ chip ^ away]
        outs[away][...] = found.astype(outs[away].dtype)


def update_kernel(sz, last, *refs):
    parts = refs[: sz.chips]
    balances, lam, shed, loads, gens, select, costs, dual, previous, cap, commit = refs[sz.chips : sz.chips + 11]
    rest = refs[sz.chips + 11 :]
    core = where_am_i()[2]
    balance = jnp.where(core == 0, balances[: sz.rows, :1], balances[sz.rows :, :1])
    lam_now = lam[:, :1]
    shift = balance + lam_now
    shift = jnp.concatenate([shift] * sz.fold, 0)
    total = parts[0][...]
    for part in parts[1:]:
        total = total + part[...].astype(F32)
    grad = total + shift
    capacity = cap[...] * commit[...].astype(F32)
    if last:
        weights, gens_out, shed_out, lam_out, weighted_out, dual_out = rest
    else:
        gens_out, shed_out, lam_out, inject = rest
    lam_out[...] = jnp.broadcast_to(lam_now + balance, lam_out.shape)
    piles = [stacked(grad[fold * sz.rows : (fold + 1) * sz.rows]) for fold in range(sz.fold)]
    picked = [
        unstacked(jnp.dot(piles[rows.start // sz.rows][:, cols], select[block], preferred_element_type=F32), sz.rows)
        for block, rows, cols in blocks_of(sz)
    ]
    picked = jnp.concatenate(picked, 1)
    now = gens[...]
    gen_grad = costs[:1] + costs[1:] * now + dual[...] + (now - previous[...]) + picked
    now = jnp.minimum(jnp.maximum(now - 0.4 * gen_grad, 0.0), capacity)
    gens_out[...] = now
    if last:
        dual_out[...] = dual[...] + now
        weighted_out[:1] = jnp.sum(weights[:, :1] * now, axis=0, keepdims=True)
        all_weights = jnp.sum(weights[:, :1], axis=0, keepdims=True)
        weighted_out[1:] = jnp.broadcast_to(all_weights, (7, sz.gens))
    else:
        placed = place(sz, now, select)
    for block, rows, cols in blocks_of(sz):
        buses = slice(block * sz.width, (block + 1) * sz.width)
        load = loads[:, buses]
        shed_next = jnp.minimum(jnp.maximum(shed[:, buses] - 0.4 * (1.5 + grad[rows, cols]), 0.0), load)
        shed_out[:, buses] = shed_next
        if not last:
            inject[rows, cols] = (placed[block] + shed_next - load).astype(BF)


def add_kernel(first, second, out):
    out[...] = first[...] + second[...]


def finish_kernel(sz, *refs):
    parts = refs[: sz.chips]
    dual, consensus, dual_out = refs[sz.chips :]
    total = parts[0][...]
    for part in parts[1:]:
        total = total + part[...]
    mean = total[:1] / total[1:2]
    consensus[...] = mean
    dual_out[...] = dual[...] - mean


def to_scen(n, away, value):
    return lax.ppermute(value, "scen", [(i, i ^ away) for i in range(n)])


def to_chip(n, away, value):
    return lax.ppermute(value, "line", [(i, i ^ (2 * away)) for i in range(n)])


def spread(move, n, values):
    found = {away: move(n, away, values[away - 1]) for away in range(1, len(values) + 1)}
    return [found[away] for away in range(1, len(values) + 1)]


def to_core(n, value):
    return lax.ppermute(value, "line", [(i, i ^ 1) for i in range(n)])


def local(
    mesh,
    shift_factors,
    gen_bus,
    commit,
    cost_coef,
    gen_cap,
    bus_loads,
    load_shed,
    dispatch,
    ph_dual,
    consensus_prev,
    scen_weight,
    flow_copy,
    flow_dual,
    balance_dual,
    flow_limit,
):
    lines, buses = shift_factors.shape
    rows, gens = dispatch.shape
    sz = Sizes(mesh, lines, buses, gens, rows)
    n_scen, n_line, chips = sz.scen, sz.line, sz.chips
    row = lambda v: v.reshape(1, -1)
    column = lambda v: jnp.broadcast_to(v[:, None], (rows, LANES))
    capacity, on, previous, limits = row(gen_cap), row(commit), row(consensus_prev), row(flow_limit)
    lam, weights = column(balance_dual), column(scen_weight)
    packed = (sz.fold * rows, sz.part)
    step_b = next(s for s in (1024, 640, 512, 256, 128) if buses % s == 0)
    macs = [sz.total * 2 * half * buses for half in sz.halves]

    generation, copies, duals = dispatch, flow_copy, flow_dual
    first = (dispatch, load_shed - bus_loads, row(gen_bus))
    made = ((packed, BF), ((gens // LANES, sz.width, LANES), BF))
    shed = load_shed
    inject, select = call(
        functools.partial(start_kernel, sz),
        first,
        made,
        flops=1000 * lines * buses,
        limit=GRANT - nbytes(first + tuple(jax.ShapeDtypeStruct(*each) for each in made)) - (1 << 16),
    )
    for iteration in range(ITERS):
        own = [inject] + spread(to_chip, n_line, [inject] * (chips - 1))
        other = [to_core(n_line, value) for value in own]
        final = iteration == ITERS - 1
        tall = 2 * sz.pair
        widths = (sz.halves[0] + LANES, sz.halves[1])
        flows = []
        for chunk in range(CHUNKS):
            block = (tall, widths[chunk])
            flows.append(
                call(
                    functools.partial(forward_kernel, sz, chunk),
                    (*own, *other, shift_factors),
                    [(block, F32)] + [(block, BF)] * (n_scen - 1),
                    [((sz.total, buses), BF), ((chips, *block), F32)],
                    flops=2 * macs[chunk],
                    limit=GRANT - (nbytes(own + other) if iteration == 0 else 0),
                )
            )
            if chunk == 0:
                parts = [flows[0][0]] + spread(to_scen, n_scen, flows[0][1:])
        state = lambda width: [((sz.pair, width), F32)] * 2
        old = (flow_copy, flow_dual) if iteration == 0 else None
        first_res, rest, first_copy, first_dual = call(
            functools.partial(residual_kernel, sz, 0),
            (*parts, *(old or (copies[0], duals[0])), limits, flows[1][0]),
            [
                ((tall, sz.early + LANES), BF),
                ((tall, sz.halves[0] - sz.early), BF),
                *state(2 * sz.halves[0]),
            ],
            keep=shift_factors,
        )
        got = spread(to_scen, n_scen, flows[1][1:])
        second_res, second_copy, second_dual = call(
            functools.partial(residual_kernel, sz, 1),
            (
                flows[1][0],
                *got,
                *(old or (copies[1], duals[1])),
                limits,
                rest,
            ),
            [((tall, lines // 2 - sz.early), BF), *state(2 * sz.halves[1])],
            keep=shift_factors,
        )
        residuals = [
            [first_res] + spread(to_scen, n_scen, [first_res] * (n_scen - 1)),
            [second_res] + spread(to_scen, n_scen, [second_res] * (n_scen - 1)),
        ]
        new_copies, new_duals = [first_copy, second_copy], [first_dual, second_dual]
        copies, duals = new_copies, new_duals
        before, balances = (), None
        for chunk in range(CHUNKS):
            last = chunk == CHUNKS - 1
            half = (sz.total // 2, buses)
            outs = [(half, F32), (half, BF)] if last else [((sz.total, buses), F32)]
            if chunk == 0:
                outs.append(((sz.pair, LANES), F32))
            found = call(
                functools.partial(backward_kernel, sz, chunk, step_b),
                (*residuals[chunk], shift_factors, *before),
                outs,
                [((sz.total, sum(high - low for low, high in sz.ranges[chunk])), BF)],
                flops=sum(macs),
            )
            if chunk == 0:
                balances = found[-1]
            before = found[:1]
        kept, sent = found[:2]
        sums = call(
            functools.partial(chip_kernel, sz),
            (kept, to_core(n_line, sent)),
            [(packed, F32)] + [(packed, BF)] * (chips - 1),
            [((chips, *packed), F32)],
            keep=None if final else shift_factors,
        )
        parts = [sums[0]] + spread(to_chip, n_line, sums[1:])
        args = (*parts, balances, lam, shed, bus_loads, generation, select, cost_coef, ph_dual, previous, capacity, on)
        if not final:
            generation, shed, lam, inject = call(
                functools.partial(update_kernel, sz, False),
                args,
                [((rows, gens), F32), ((rows, buses), F32), ((rows, LANES), F32), (packed, BF)],
                keep=shift_factors,
                limit=GRANT - nbytes((dispatch, select)),
            )
        else:
            generation, shed, lam, weighted, dual_sum = call(
                functools.partial(update_kernel, sz, True),
                (*args, weights),
                [((rows, gens), F32), ((rows, buses), F32), ((rows, LANES), F32), ((8, gens), F32), ((rows, gens), F32)],
            )
    (weighted,) = call(add_kernel, (weighted, to_core(n_line, weighted)), [((8, gens), F32)])
    parts = [weighted] + spread(to_chip, n_line, [weighted] * (chips - 1))
    consensus, dual_out = call(
        functools.partial(finish_kernel, sz),
        (*parts, dual_sum),
        [((1, gens), F32), ((rows, gens), F32)],
    )
    return generation, shed, jnp.concatenate(copies, 1), jnp.concatenate(duals, 1), lam[:, 0], consensus.reshape(-1), dual_out


def solution(mesh):
    return jax.shard_map(
        functools.partial(local, mesh),
        mesh=mesh,
        in_specs=(
            P("line", "scen"),
            P("scen"),
            P("scen"),
            P(None, "scen"),
            P("scen"),
            P("line", "scen"),
            P("line", "scen"),
            P("line", "scen"),
            P("line", "scen"),
            P("scen"),
            P("line"),
            P("scen", "line"),
            P("scen", "line"),
            P("line"),
            P("line"),
        ),
        out_specs=(
            P("line", "scen"),
            P("line", "scen"),
            P("scen", "line"),
            P("scen", "line"),
            P("line"),
            P("scen"),
            P("line", "scen"),
        ),
        check_vma=False,
    )
```

```python
import functools
import math

import jax
import jax.numpy as jnp
from jax import lax
from jax.experimental import pallas as pl
from jax.experimental.pallas import tpu as pltpu
from jax.sharding import PartitionSpec as P

BUSES = 20480
ITERS = 2
CHUNKS = 2
FIRST_SHARE = 0.5
EARLY_SHARE = 0.4375
LANES = 128
GRANT = 11 << 20
BF = jnp.bfloat16
F32 = jnp.float32
WHOLE = pl.BlockSpec(memory_space=pltpu.VMEM)


def call(kernel, args, outs, scratch=(), flops=0, keep=None, limit=GRANT):
    size = sum(a.size * a.dtype.itemsize for a in args)
    if keep is not None:
        inner, args = kernel, (keep, *args)
        kernel = lambda kept, *refs: inner(*refs)
    return pl.pallas_call(
        kernel,
        in_specs=[WHOLE] * len(args),
        out_specs=[WHOLE] * len(outs),
        out_shape=[jax.ShapeDtypeStruct(shape, kind) for shape, kind in outs],
        scratch_shapes=[pltpu.VMEM(shape, kind) for shape, kind in scratch],
        compiler_params=pltpu.CompilerParams(vmem_limit_bytes=limit),
        cost_estimate=pl.CostEstimate(flops=flops, bytes_accessed=size, transcendentals=0),
    )(*args)


def nbytes(arrays):
    size = lambda a: math.prod(a.shape[:-2]) * -(-a.shape[-2] // 8) * 8 * a.shape[-1] * a.dtype.itemsize
    return sum(size(a) for a in arrays)


def pieces(value):
    high = value.astype(BF)
    rest = value - high.astype(F32)
    middle = rest.astype(BF)
    low = (rest - middle.astype(F32)).astype(BF)
    return high, middle, low


def stacked(value):
    rows, columns = value.shape
    below = [jnp.zeros((8 - rows, columns), F32)] if rows < 8 else []
    parts = []
    for piece in pieces(value):
        parts += [piece.astype(F32)] + below
    return jnp.concatenate(parts, 0).astype(BF)


def unstacked(product, rows):
    return (product[16 : 16 + rows] + product[8 : 8 + rows]) + product[:rows]


def dot_t(a, b):
    return lax.dot_general(a, b, (((1,), (1,)), ((), ())), preferred_element_type=F32)


class Sizes:
    def __init__(self, mesh, lines, buses, gens, rows):
        self.scen = mesh.shape["scen"]
        self.line = mesh.shape["line"]
        self.chips = self.line // 2
        assert self.chips == self.scen
        self.lines, self.buses, self.gens, self.rows = lines, buses, gens, rows
        self.pair = 2 * rows
        self.total = rows * self.line
        self.stretch = buses // gens
        self.width = self.stretch * LANES
        self.fold = next(f for f in (4, 2, 1) if buses % (f * self.width) == 0)
        self.part = buses // self.fold
        self.pack = next(p for p in (4, 2, 1) if gens % (p * LANES) == 0)
        tiles = lambda share, least, most: min(max(round(share * lines / 2 / LANES), least), most) * LANES
        first = tiles(FIRST_SHARE, 2, lines // 2 // LANES - 1)
        self.halves = (first, lines // 2 - first)
        self.early = tiles(EARLY_SHARE, 1, first // LANES - 1)
        self.starts = (0, 2 * first)
        self.ranges = (((0, self.early), (first, first + self.early)), ((self.early, first), (first + self.early, lines)))


def where_am_i():
    line = lax.axis_index("line")
    return lax.axis_index("scen"), lax.div(line, 2), lax.rem(line, 2)


def place(sz, gens, select):
    pile = stacked(gens)
    blocks = [dot_t(pile[:, block * LANES : (block + 1) * LANES], select[block]) for block in range(sz.gens // LANES)]
    return [unstacked(product, sz.rows) for product in blocks]


def blocks_of(sz):
    per = sz.part // sz.width
    for block in range(sz.gens // LANES):
        fold, inner = divmod(block, per)
        yield block, slice(fold * sz.rows, (fold + 1) * sz.rows), slice(inner * sz.width, (inner + 1) * sz.width)


def start_kernel(sz, dispatch, net, gen_bus, inject, select):
    first = lax.axis_index("scen") * sz.buses
    bus = lax.broadcasted_iota(jnp.int32, (sz.width, LANES), 0)
    for block, rows, cols in blocks_of(sz):
        lanes = slice(block * LANES, (block + 1) * LANES)
        local = gen_bus[:, lanes] - (first + block * sz.width)
        select[block] = (bus == local).astype(F32).astype(BF)
    placed = place(sz, dispatch[...], select)
    for block, rows, cols in blocks_of(sz):
        inject[rows, cols] = (placed[block] + net[:, block * sz.width : (block + 1) * sz.width]).astype(BF)


def forward_kernel(sz, chunk, *refs):
    chips = sz.chips
    own, other = refs[:chips], refs[chips : 2 * chips]
    factors = refs[2 * chips]
    outs = refs[2 * chips + 1 : 3 * chips + 1]
    inject, flows = refs[3 * chips + 1 :]
    scen, chip, core = where_am_i()
    half = sz.halves[chunk]

    def gather(first, second):
        for slot in range(chips):
            for fold in range(sz.fold):
                rows = slice(fold * sz.rows, (fold + 1) * sz.rows)
                cols = slice(fold * sz.part, (fold + 1) * sz.part)
                base = slot * sz.pair
                inject[base : base + sz.rows, cols] = first[slot][rows, :]
                inject[base + sz.rows : base + sz.pair, cols] = second[slot][rows, :]

    @pl.when(core == 0)
    def _():
        gather(own, other)

    @pl.when(core == 1)
    def _():
        gather(other, own)

    if chunk == 0:
        total = jnp.sum(inject[...].astype(F32), axis=1, keepdims=True)
        high, middle, low = (piece.astype(F32) for piece in pieces(total))
        lane = lax.broadcasted_iota(jnp.int32, (sz.total, LANES), 1)
        tile = jnp.where(lane == 0, high, jnp.where(lane == 1, middle, jnp.where(lane == 2, low, 0.0)))
        for slot in range(chips):
            flows[slot, :, half:] = jnp.zeros((2 * sz.pair, LANES), F32)
            flows[slot, : sz.pair, half:] = tile[slot * sz.pair : (slot + 1) * sz.pair]
    for side in range(2):
        start = sz.starts[chunk] + side * half
        product = dot_t(factors[start : start + half, :], inject[...]).T
        for slot in range(chips):
            flows[slot, side * sz.pair : (side + 1) * sz.pair, :half] = product[slot * sz.pair : (slot + 1) * sz.pair]
    for away in range(chips):
        found = flows[chip ^ scen ^ away]
        outs[away][...] = found.astype(outs[away].dtype)


def residual_kernel(sz, chunk, *refs):
    scen = sz.scen
    half, early, start = sz.halves[chunk], sz.early, sz.starts[chunk]
    parts = refs[:scen]
    copies, duals, limits = refs[scen : scen + 3]
    if chunk == 0:
        residual, rest, copy_out, dual_out = refs[scen + 4 :]
    else:
        rest, residual, copy_out, dual_out = refs[scen + 3 :]
        before = rest.shape[1]
        residual[:, :before] = rest[...]
    total = parts[0][...]
    for part in parts[1:]:
        total = total + part[...].astype(F32)
    for side in range(2):
        rows = slice(side * sz.pair, (side + 1) * sz.pair)
        base = start if copies.shape[1] == sz.lines else 0
        cols = slice(base + side * half, base + (side + 1) * half)
        to = slice(side * half, (side + 1) * half)
        now, copy, dual = total[rows, :half], copies[:, cols], duals[:, cols]
        limit = limits[:, start + side * half : start + (side + 1) * half]
        found = (now - copy + dual).astype(BF)
        if chunk == 0:
            residual[rows, :early] = found[:, :early]
            rest[rows, :] = found[:, early:]
        else:
            residual[rows, before:] = found
        copy_next = jnp.minimum(jnp.maximum(now + dual, -limit), limit)
        copy_out[:, to] = copy_next
        dual_out[:, to] = dual + now - copy_next
    if chunk == 0:
        balance = jnp.sum(total[:, half:], axis=1, keepdims=True) / BUSES
        high, middle, low = (piece.astype(F32) for piece in pieces(balance))
        lane = lax.broadcasted_iota(jnp.int32, (2 * sz.pair, LANES), 1)
        tile = jnp.where(lane == 0, high, jnp.where(lane == 1, middle, jnp.where(lane == 2, low, 0.0)))
        residual[:, early:] = tile.astype(BF)


def backward_kernel(sz, chunk, step, *refs):
    scen = sz.scen
    parts, factors = refs[:scen], refs[scen]
    before = refs[scen + 1] if chunk else None
    last = chunk == CHUNKS - 1
    residual = refs[-1]
    outs = refs[scen + 1 + (chunk > 0) : -1]
    me, chip, core = where_am_i()
    if chunk == 0:
        balances = outs[-1]
        for slot in range(scen):

            @pl.when(chip == (me ^ slot))
            def _(slot=slot):
                tile = parts[slot][: sz.pair, sz.early : sz.early + LANES].astype(F32)
                found = jnp.sum(tile, axis=1, keepdims=True)
                balances[...] = jnp.broadcast_to(found, (sz.pair, LANES))

    widths = (sz.early,) if chunk == 0 else (sz.halves[0] - sz.early, sz.halves[1])
    for slot in range(scen):
        source = target = 0
        for width in widths:
            for side in range(2):
                residual[slot * sz.pair : (slot + 1) * sz.pair, target : target + width] = parts[slot][
                    side * sz.pair : (side + 1) * sz.pair, source : source + width
                ]
                target += width
            source += width

    def body(i, _):
        cols = pl.ds(pl.multiple_of(i * step, step), step)
        product, at = None, 0
        for low, high in sz.ranges[chunk]:
            term = jnp.dot(
                residual[:, at : at + high - low], factors[low:high, cols], preferred_element_type=F32
            )
            product = term if product is None else product + term
            at += high - low
        if chunk:
            product = before[:, cols] + product
        if not last:
            outs[0][:, cols] = product
            return 0
        kept, sent = outs[:2]
        even = [product[slot * sz.pair : slot * sz.pair + sz.rows] for slot in range(scen)]
        odd = [product[slot * sz.pair + sz.rows : (slot + 1) * sz.pair] for slot in range(scen)]
        even, odd = jnp.concatenate(even, 0), jnp.concatenate(odd, 0)
        kept[:, cols] = jnp.where(core == 0, even, odd)
        sent[:, cols] = jnp.where(core == 0, odd, even).astype(BF)
        return 0

    lax.fori_loop(0, sz.buses // step, body, 0)


def chip_kernel(sz, *refs):
    kept, received = refs[:2]
    outs, packed = refs[2:-1], refs[-1]
    scen, chip, core = where_am_i()
    total = kept[...] + received[...].astype(F32)
    for slot in range(sz.scen):
        for fold in range(sz.fold):
            packed[slot, fold * sz.rows : (fold + 1) * sz.rows, :] = total[
                slot * sz.rows : (slot + 1) * sz.rows, fold * sz.part : (fold + 1) * sz.part
            ]
    for away in range(sz.chips):
        found = packed[scen ^ chip ^ away]
        outs[away][...] = found.astype(outs[away].dtype)


def update_kernel(sz, last, *refs):
    parts = refs[: sz.chips]
    balances, lam, shed, loads, gens, select, costs, dual, previous, cap, commit = refs[sz.chips : sz.chips + 11]
    rest = refs[sz.chips + 11 :]
    core = where_am_i()[2]
    balance = jnp.where(core == 0, balances[: sz.rows, :1], balances[sz.rows :, :1])
    lam_now = lam[:, :1]
    shift = balance + lam_now
    shift = jnp.concatenate([shift] * sz.fold, 0)
    total = parts[0][...]
    for part in parts[1:]:
        total = total + part[...].astype(F32)
    grad = total + shift
    capacity = cap[...] * commit[...].astype(F32)
    if last:
        weights, gens_out, shed_out, lam_out, weighted_out, dual_out = rest
    else:
        gens_out, shed_out, lam_out, inject = rest
    lam_out[...] = jnp.broadcast_to(lam_now + balance, lam_out.shape)
    piles = [stacked(grad[fold * sz.rows : (fold + 1) * sz.rows]) for fold in range(sz.fold)]
    picked = [
        unstacked(jnp.dot(piles[rows.start // sz.rows][:, cols], select[block], preferred_element_type=F32), sz.rows)
        for block, rows, cols in blocks_of(sz)
    ]
    picked = jnp.concatenate(picked, 1)
    now = gens[...]
    gen_grad = costs[:1] + costs[1:] * now + dual[...] + (now - previous[...]) + picked
    now = jnp.minimum(jnp.maximum(now - 0.4 * gen_grad, 0.0), capacity)
    gens_out[...] = now
    if last:
        dual_out[...] = dual[...] + now
        weighted = jnp.sum(weights[:, :1] * now, axis=0, keepdims=True)
        all_weights = jnp.sum(weights[:, :1], axis=0, keepdims=True)
        weighted_out[sz.pack :] = jnp.broadcast_to(all_weights, (8 - sz.pack, sz.gens // sz.pack))
        for i in range(sz.pack):
            weighted_out[i : i + 1] = weighted[:, i * sz.gens // sz.pack : (i + 1) * sz.gens // sz.pack]
    else:
        placed = place(sz, now, select)
    for block, rows, cols in blocks_of(sz):
        buses = slice(block * sz.width, (block + 1) * sz.width)
        load = loads[:, buses]
        shed_next = jnp.minimum(jnp.maximum(shed[:, buses] - 0.4 * (1.5 + grad[rows, cols]), 0.0), load)
        shed_out[:, buses] = shed_next
        if not last:
            inject[rows, cols] = (placed[block] + shed_next - load).astype(BF)


def add_kernel(first, second, out):
    out[...] = first[...] + second[...]


def finish_kernel(sz, *refs):
    parts = refs[: sz.chips]
    dual, consensus, dual_out = refs[sz.chips :]
    total = parts[0][...]
    for part in parts[1:]:
        total = total + part[...]
    mean = jnp.concatenate([total[i : i + 1] / total[sz.pack : sz.pack + 1] for i in range(sz.pack)], 1)
    consensus[...] = mean
    dual_out[...] = dual[...] - mean


def to_scen(n, away, value):
    return lax.ppermute(value, "scen", [(i, i ^ away) for i in range(n)])


def to_chip(n, away, value):
    return lax.ppermute(value, "line", [(i, i ^ (2 * away)) for i in range(n)])


def spread(move, n, values):
    found = {away: move(n, away, values[away - 1]) for away in range(1, len(values) + 1)}
    return [found[away] for away in range(1, len(values) + 1)]


def to_core(n, value):
    return lax.ppermute(value, "line", [(i, i ^ 1) for i in range(n)])


def local(
    mesh,
    shift_factors,
    gen_bus,
    commit,
    cost_coef,
    gen_cap,
    bus_loads,
    load_shed,
    dispatch,
    ph_dual,
    consensus_prev,
    scen_weight,
    flow_copy,
    flow_dual,
    balance_dual,
    flow_limit,
):
    lines, buses = shift_factors.shape
    rows, gens = dispatch.shape
    sz = Sizes(mesh, lines, buses, gens, rows)
    n_scen, n_line, chips = sz.scen, sz.line, sz.chips
    row = lambda v: v.reshape(1, -1)
    column = lambda v: jnp.broadcast_to(v[:, None], (rows, LANES))
    capacity, on, previous, limits = row(gen_cap), row(commit), row(consensus_prev), row(flow_limit)
    lam, weights = column(balance_dual), column(scen_weight)
    packed = (sz.fold * rows, sz.part)
    step_b = next(s for s in (1024, 640, 512, 256, 128) if buses % s == 0)
    macs = [sz.total * 2 * half * buses for half in sz.halves]

    generation, copies, duals = dispatch, flow_copy, flow_dual
    first = (dispatch, load_shed - bus_loads, row(gen_bus))
    made = ((packed, BF), ((gens // LANES, sz.width, LANES), BF))
    shed = load_shed
    inject, select = call(
        functools.partial(start_kernel, sz),
        first,
        made,
        flops=1000 * lines * buses,
        limit=GRANT - nbytes(first + tuple(jax.ShapeDtypeStruct(*each) for each in made)) - (1 << 16),
    )
    for iteration in range(ITERS):
        own = [inject] + spread(to_chip, n_line, [inject] * (chips - 1))
        other = [to_core(n_line, value) for value in own]
        final = iteration == ITERS - 1
        tall = 2 * sz.pair
        widths = (sz.halves[0] + LANES, sz.halves[1])
        flows = []
        for chunk in range(CHUNKS):
            block = (tall, widths[chunk])
            flows.append(
                call(
                    functools.partial(forward_kernel, sz, chunk),
                    (*own, *other, shift_factors),
                    [(block, F32)] + [(block, BF)] * (n_scen - 1),
                    [((sz.total, buses), BF), ((chips, *block), F32)],
                    flops=2 * macs[chunk],
                    limit=GRANT - (nbytes(own + other) if iteration == 0 else 0),
                )
            )
            if chunk == 0:
                parts = [flows[0][0]] + spread(to_scen, n_scen, flows[0][1:])
        state = lambda width: [((sz.pair, width), F32)] * 2
        old = (flow_copy, flow_dual) if iteration == 0 else None
        first_res, rest, first_copy, first_dual = call(
            functools.partial(residual_kernel, sz, 0),
            (*parts, *(old or (copies[0], duals[0])), limits, flows[1][0]),
            [
                ((tall, sz.early + LANES), BF),
                ((tall, sz.halves[0] - sz.early), BF),
                *state(2 * sz.halves[0]),
            ],
            keep=shift_factors,
        )
        got = spread(to_scen, n_scen, flows[1][1:])
        second_res, second_copy, second_dual = call(
            functools.partial(residual_kernel, sz, 1),
            (
                flows[1][0],
                *got,
                *(old or (copies[1], duals[1])),
                limits,
                rest,
            ),
            [((tall, lines // 2 - sz.early), BF), *state(2 * sz.halves[1])],
            keep=shift_factors,
        )
        residuals = [
            [first_res] + spread(to_scen, n_scen, [first_res] * (n_scen - 1)),
            [second_res] + spread(to_scen, n_scen, [second_res] * (n_scen - 1)),
        ]
        new_copies, new_duals = [first_copy, second_copy], [first_dual, second_dual]
        copies, duals = new_copies, new_duals
        before, balances = (), None
        for chunk in range(CHUNKS):
            last = chunk == CHUNKS - 1
            half = (sz.total // 2, buses)
            outs = [(half, F32), (half, BF)] if last else [((sz.total, buses), F32)]
            if chunk == 0:
                outs.append(((sz.pair, LANES), F32))
            found = call(
                functools.partial(backward_kernel, sz, chunk, step_b),
                (*residuals[chunk], shift_factors, *before),
                outs,
                [((sz.total, sum(high - low for low, high in sz.ranges[chunk])), BF)],
                flops=sum(macs),
            )
            if chunk == 0:
                balances = found[-1]
            before = found[:1]
        kept, sent = found[:2]
        sums = call(
            functools.partial(chip_kernel, sz),
            (kept, to_core(n_line, sent)),
            [(packed, F32)] + [(packed, BF)] * (chips - 1),
            [((chips, *packed), F32)],
            keep=None if final else shift_factors,
        )
        parts = [sums[0]] + spread(to_chip, n_line, sums[1:])
        args = (*parts, balances, lam, shed, bus_loads, generation, select, cost_coef, ph_dual, previous, capacity, on)
        if not final:
            generation, shed, lam, inject = call(
                functools.partial(update_kernel, sz, False),
                args,
                [((rows, gens), F32), ((rows, buses), F32), ((rows, LANES), F32), (packed, BF)],
                keep=shift_factors,
                limit=GRANT - nbytes((dispatch, select)),
            )
        else:
            generation, shed, lam, weighted, dual_sum = call(
                functools.partial(update_kernel, sz, True),
                (*args, weights),
                [((rows, gens), F32), ((rows, buses), F32), ((rows, LANES), F32), ((8, gens // sz.pack), F32), ((rows, gens), F32)],
            )
    (weighted,) = call(add_kernel, (weighted, to_core(n_line, weighted)), [((8, gens // sz.pack), F32)])
    parts = [weighted] + spread(to_chip, n_line, [weighted] * (chips - 1))
    consensus, dual_out = call(
        functools.partial(finish_kernel, sz),
        (*parts, dual_sum),
        [((1, gens), F32), ((rows, gens), F32)],
    )
    return generation, shed, jnp.concatenate(copies, 1), jnp.concatenate(duals, 1), lam[:, 0], consensus.reshape(-1), dual_out


def solution(mesh):
    return jax.shard_map(
        functools.partial(local, mesh),
        mesh=mesh,
        in_specs=(
            P("line", "scen"),
            P("scen"),
            P("scen"),
            P(None, "scen"),
            P("scen"),
            P("line", "scen"),
            P("line", "scen"),
            P("line", "scen"),
            P("line", "scen"),
            P("scen"),
            P("line"),
            P("scen", "line"),
            P("scen", "line"),
            P("line"),
            P("line"),
        ),
        out_specs=(
            P("line", "scen"),
            P("line", "scen"),
            P("scen", "line"),
            P("scen", "line"),
            P("line"),
            P("scen"),
            P("line", "scen"),
        ),
        check_vma=False,
    )
```
